32 devices in a mesh: gx: 8 (over z, y), gy: 4 (over x, core).
Axes of the slice: x: 2, y: 2, z: 4, core: 2. Of those that a mesh axis runs over, the one named last changes fastest.
Arguments:
- hamiltonian: bfloat16 [32, 16, 64, 576], P('gx', 'gy'), as said below
- density: bfloat16 [32, 16, 64, 576], P('gx', 'gy'), as said below
- block_pattern: int32 [32, 16, 9], P('gx', 'gy'), may hold values from 0 to 1, as said below
- filter_mask: int32 [32, 16, 9], P('gx', 'gy'), may hold values from 0 to 1, as said below
Outputs:
- gradient: bfloat16 [32, 16, 64, 576], P('gx', 'gy')
The draws below stay inside these ranges and needn't reach their ends.
Inputs may be any that keep to these rules, and one draw needn't show every extreme that they name: `block_pattern`: Symmetric: the value at block row i and slot k equals the value at block row i + s_k and slot 8 - k; the middle slot (k = 4) is always 1. `filter_mask`: Symmetric: the value at block row i and slot k equals the value at block row i + s_k and slot 8 - k; the middle slot (k = 4) is always 1. `hamiltonian`: A symmetric matrix: block (i, k) is the transpose of block (i + s_k, 8 - k), and every middle block (k = 4) is symmetric. `density`: A symmetric matrix: block (i, k) is the transpose of block (i + s_k, 8 - k), and every middle block (k = 4) is symmetric.
All inputs are finite; a program needn't handle non-finite values.
Results may differ from the reference program's by a relative error of at most 0.006.
Values may be sent and summed in bfloat16 or wider, within the bound.
No kernel may reach another device: no remote copies, remote signals or barrier semaphores. Data moves between devices by JAX's collectives and lax.ppermute only.
A program may use at most 192 MiB of HBM per device.

```python
import jax
import jax.numpy as jnp

BS = 64
GXB = 32
GYB = 16


def symmetric_mask(key, salt):
    base = jax.random.randint(jax.random.fold_in(key, salt), (GXB, GYB, 9), 0, 4)
    live = (base != 0).astype(jnp.int32)
    columns = []
    for slot_index in range(9):
        if slot_index == 4:
            columns.append(jnp.ones((GXB, GYB), jnp.int32))
        elif slot_index > 4:
            columns.append(live[:, :, slot_index])
        else:
            shift_x = slot_index // 3 - 1
            shift_y = slot_index % 3 - 1
            columns.append(jnp.roll(live[:, :, 8 - slot_index], (-shift_x, -shift_y), axis=(0, 1)))
    return jnp.stack(columns, axis=-1)


def symmetric_strips(key, scale, limit):
    shape = (GXB, GYB, BS, 9 * BS)
    base = jax.random.normal(key, shape, jnp.float32)
    base = jnp.clip(base * scale, -limit, limit)
    blocks = base.reshape(GXB, GYB, BS, 9, BS)
    columns = []
    for slot_index in range(9):
        if slot_index == 4:
            middle = blocks[:, :, :, 4, :]
            columns.append((middle + jnp.swapaxes(middle, 2, 3)) * 0.5)
        elif slot_index > 4:
            columns.append(blocks[:, :, :, slot_index, :])
        else:
            shift_x = slot_index // 3 - 1
            shift_y = slot_index % 3 - 1
            source = blocks[:, :, :, 8 - slot_index, :]
            moved = jnp.roll(source, (-shift_x, -shift_y), axis=(0, 1))
            columns.append(jnp.swapaxes(moved, 2, 3))
    return jnp.stack(columns, axis=3).reshape(shape)


def draw_hamiltonian(key, part):
    return symmetric_strips(jax.random.fold_in(key, 31), 0.4, 2.5).astype(jnp.bfloat16)


def draw_density(key, part):
    scale = (3.0 * BS) ** (-0.5)
    return symmetric_strips(jax.random.fold_in(key, 47), scale, 6.0 * scale).astype(jnp.bfloat16)


def draw_block_pattern(key, part):
    return symmetric_mask(key, 11)


def draw_filter_mask(key, part):
    return symmetric_mask(key, 23)


def setup_inputs(seed: int = 0) -> dict:
    keys = jax.random.split(jax.random.key(seed), 5)
    return {
        "hamiltonian": draw_hamiltonian(jax.random.fold_in(keys[4], 71), 0),
        "density": draw_density(jax.random.fold_in(keys[4], 71), 0),
        "block_pattern": draw_block_pattern(jax.random.fold_in(keys[4], 71), 0),
        "filter_mask": draw_filter_mask(jax.random.fold_in(keys[4], 71), 0),
    }


def pair_list(target):
    target_x = target // 3 - 1
    target_y = target % 3 - 1
    pairs = []
    for source in range(9):
        move_x = source // 3 - 1
        move_y = source % 3 - 1
        rest_x = target_x - move_x
        rest_y = target_y - move_y
        if abs(rest_x) <= 1 and abs(rest_y) <= 1:
            pairs.append((source, (rest_x + 1) * 3 + rest_y + 1, move_x, move_y))
    return pairs


def block_mask(strips, mask, width):
    shape = strips.shape
    split = strips.reshape(shape[0], shape[1], width, 9, width)
    split = split * mask[:, :, None, :, None].astype(strips.dtype)
    return split.reshape(shape)


def stencil_product(left, right, margin, width):
    rows_x = left.shape[0]
    rows_y = left.shape[1]
    outputs = []
    for target in range(9):
        lefts = []
        rights = []
        for source, inner, move_x, move_y in pair_list(target):
            lefts.append(left[:, :, :, source * width:(source + 1) * width])
            moved = right[margin + move_x:margin + move_x + rows_x, margin + move_y:margin + move_y + rows_y]
            rights.append(moved[:, :, :, inner * width:(inner + 1) * width])
        joined_left = jnp.concatenate(lefts, axis=-1).astype(jnp.float32)
        joined_right = jnp.concatenate(rights, axis=-2).astype(jnp.float32)
        outputs.append(jnp.einsum("xyab,xybc->xyac", joined_left, joined_right))
    return jnp.concatenate(outputs, axis=-1)


def wrap_pad(strips):
    return jnp.pad(strips, ((1, 1), (1, 1), (0, 0), (0, 0)), mode="wrap")


def transposed(padded, rows_x, rows_y, width):
    blocks = []
    for target in range(9):
        move_x = target // 3 - 1
        move_y = target % 3 - 1
        moved = padded[1 + move_x:1 + move_x + rows_x, 1 + move_y:1 + move_y + rows_y]
        piece = moved[:, :, :, (8 - target) * width:(9 - target) * width]
        blocks.append(jnp.swapaxes(piece, 2, 3))
    return jnp.concatenate(blocks, axis=-1)


def reference(hamiltonian, density, block_pattern, filter_mask):
    width = BS
    rows_x = hamiltonian.shape[0]
    rows_y = hamiltonian.shape[1]
    ham_masked = block_mask(hamiltonian, block_pattern, width)
    dens_masked = block_mask(density, block_pattern, width)
    dens_pad = wrap_pad(dens_masked)
    hp = block_mask(stencil_product(ham_masked, dens_pad, 1, width), filter_mask, width).astype(jnp.bfloat16)
    hpp = block_mask(stencil_product(hp, dens_pad, 1, width), filter_mask, width).astype(jnp.bfloat16)
    hp_pad = wrap_pad(hp)
    php = block_mask(stencil_product(dens_masked, hp_pad, 1, width), filter_mask, width)
    hp_turned = transposed(hp_pad, rows_x, rows_y, width)
    hpp_turned = transposed(wrap_pad(hpp), rows_x, rows_y, width)
    linear = hp.astype(jnp.float32) + hp_turned.astype(jnp.float32)
    cubic = hpp.astype(jnp.float32) + php + hpp_turned.astype(jnp.float32)
    total = block_mask(3.0 * linear - 2.0 * cubic, filter_mask, width)
    return total.astype(jnp.bfloat16)
```

```python
import functools

import jax
import jax.numpy as jnp
from jax import lax
from jax.experimental import pallas as pl
from jax.experimental.pallas import tpu as pltpu
from jax.sharding import PartitionSpec as P

W = 64
BF = jnp.bfloat16
F32 = jnp.float32
VMEM = pl.BlockSpec(memory_space=pltpu.VMEM)


def strip_mask(mask_ref, x):
    slot = lax.broadcasted_iota(jnp.int32, (9, 9 * W), 0)
    lane = lax.broadcasted_iota(jnp.int32, (9, 9 * W), 1)
    spread = (lane // W == slot).astype(BF)
    flags = mask_ref[x].astype(F32).astype(BF)
    return jnp.dot(flags, spread, preferred_element_type=F32)


def window_mask(mask_ref, x):
    slot = lax.broadcasted_iota(jnp.int32, (9, 12 * W), 0)
    lane = lax.broadcasted_iota(jnp.int32, (9, 12 * W), 1)
    flags = mask_ref[x].astype(F32).astype(BF)
    out = []
    for r in range(2):
        dy = (lane % 256) // W - r
        inside = (dy >= 0) & (dy <= 2) & (lane // 256 * 3 + dy == slot)
        out.append(jnp.dot(flags, inside.astype(BF), preferred_element_type=F32))
    return out


def put_strip(dst, x, y, strip):
    p, r = y // 2, y % 2
    for d in range(3):
        piece = strip[:, 192 * d : 192 * d + 192]
        zero = jnp.zeros((W, W), BF)
        parts = [piece, zero] if r == 0 else [zero, piece]
        dst[p, x + 1, W + W * r : 2 * W + W * r, 256 * d : 256 * d + 256] = jnp.concatenate(
            parts, axis=1
        )


def put_shared(dst, x):
    zero = jnp.zeros((W, 128), BF)
    for d in range(3):
        c = 256 * d
        dst[1, x + 1, 0:64, c : c + 128] = dst[0, x + 1, 128:192, c + 128 : c + 256]
        dst[1, x + 1, 0:64, c + 128 : c + 256] = zero
        dst[0, x + 1, 192:256, c + 128 : c + 256] = dst[1, x + 1, 64:128, c : c + 128]
        dst[0, x + 1, 192:256, c : c + 128] = zero


def put_y(dst, x, low, high):
    zero = jnp.zeros((W, 128), BF)
    for d in range(3):
        c = 256 * d
        dst[0, x + 1, 0:64, c : c + 128] = low[:, 128 * d : 128 * d + 128]
        dst[0, x + 1, 0:64, c + 128 : c + 256] = zero
        dst[1, x + 1, 192:256, c + 128 : c + 256] = high[:, 128 * d : 128 * d + 128]
        dst[1, x + 1, 192:256, c : c + 128] = zero


def put_x(dst, at, row, corner):
    z1 = jnp.zeros((W, W), BF)
    z2 = jnp.zeros((W, 128), BF)
    cell = []
    for y in range(4):
        first = row[y]
        last = row[4 + y // 2][:, W * (y % 2) : W * (y % 2) + W]
        cell.append(jnp.concatenate([first, last], axis=1))
    for p in range(2):
        a = corner[0] if p == 0 else cell[1][:, W:]
        d = corner[1] if p == 1 else cell[2][:, :128]
        tile = jnp.concatenate(
            [
                jnp.concatenate([a, z2], axis=1),
                jnp.concatenate([cell[2 * p], z1], axis=1),
                jnp.concatenate([z1, cell[2 * p + 1]], axis=1),
                jnp.concatenate([z2, d], axis=1),
            ],
            axis=0,
        )
        dst[p, at, :, 256:512] = tile
        if at == 0:
            dst[p, 0, :, 512:768] = dst[p, 1, :, 0:256].T
        else:
            dst[p, at, :, 0:256] = dst[p, at - 1, :, 512:768].T


def x_message(cells):
    out = [c[:, :128] for c in cells]
    out.append(jnp.concatenate([cells[0][:, 128:], cells[1][:, 128:]], axis=1))
    out.append(jnp.concatenate([cells[2][:, 128:], cells[3][:, 128:]], axis=1))
    return jnp.stack(out)


def pack_kernel(ham, dens, pattern, y_up, y_down, x_up, x_down):
    for x in range(4):
        mask = strip_mask(pattern, x).astype(BF)
        for n, ref in enumerate((ham, dens)):
            low = ref[x, 0] * mask[0:1]
            high = ref[x, 3] * mask[3:4]
            y_down[n, x] = jnp.concatenate([low[:, 192 * d : 192 * d + 128] for d in range(3)], axis=1)
            y_up[n, x] = jnp.concatenate(
                [high[:, 192 * d + 64 : 192 * d + 192] for d in range(3)], axis=1
            )
            if x in (0, 3):
                cells = [(ref[x, y] * mask[y : y + 1])[:, 192:384] for y in range(4)]
                out = x_down if x == 0 else x_up
                out[n] = x_message(cells)


def dense_product(left, right, p, x, e):
    total = None
    for d in range(max(-1, e - 1), min(1, e + 1) + 1):
        term = jnp.dot(
            left[:, 256 * (d + 1) : 256 * (d + 2)],
            right[p, x + 1 + d, :, 256 * (e - d + 1) : 256 * (e - d + 2)],
            preferred_element_type=F32,
        )
        total = term if total is None else total + term
    return total


def both_rows(masks, p):
    first, second = masks
    return jnp.concatenate(
        [
            jnp.broadcast_to(first[2 * p : 2 * p + 1], (W, 768)),
            jnp.broadcast_to(second[2 * p + 1 : 2 * p + 2], (W, 768)),
        ],
        axis=0,
    )


def first_kernel(
    ham, dens, pattern, kept, y_low, y_high, x_low, x_high, c_low, c_high,
    a_out, s_out, xd, sy_up, sy_down, sx_up, sx_down, xh,
):
    for n, (ref, dst) in enumerate(((ham, xh), (dens, xd))):
        for x in range(4):
            mask = strip_mask(pattern, x).astype(BF)
            for y in range(4):
                put_strip(dst, x, y, ref[x, y] * mask[y : y + 1])
            put_shared(dst, x)
            put_y(dst, x, y_low[n, x], y_high[n, x])
        put_x(dst, 0, x_low[n], c_low[n])
        put_x(dst, 5, x_high[n], c_high[n])
    for x in range(4):
        masks = window_mask(kept, x)
        for p in range(2):
            keep = both_rows(masks, p)
            lh = xh[p, x + 1, 64:192, :]
            ld = xd[p, x + 1, 64:192, :]
            for e in range(-1, 2):
                cols = slice(256 * (e + 1), 256 * (e + 2))
                a = (dense_product(lh, xd, p, x, e) * keep[:, cols]).astype(BF)
                b = (dense_product(ld, xh, p, x, e) * keep[:, cols]).astype(BF)
                a_out[p, x, :, cols] = a
                s_out[p, x, :, cols] = (a.astype(F32) + b.astype(F32)).astype(BF)
        for d in range(3):
            sy_up[x, :, 128 * d : 128 * d + 128] = s_out[1, x, 64:128, 256 * d + 128 : 256 * d + 256]
            sy_down[x, :, 128 * d : 128 * d + 128] = s_out[0, x, 0:64, 256 * d : 256 * d + 128]
    for x, out in ((0, sx_down), (3, sx_up)):
        out[...] = x_message(
            [
                s_out[y // 2, x, W * (y % 2) : W * (y % 2) + W, 256 + W * (y % 2) : 448 + W * (y % 2)]
                for y in range(4)
            ]
        )


def last_kernel(
    a_in, s_in, xd, kept, y_low, y_high, x_low, x_high, c_low, c_high, out, xs
):
    for x in range(4):
        for p in range(2):
            xs[p, x + 1, 64:192, :] = s_in[p, x]
        put_shared(xs, x)
        put_y(xs, x, y_low[x], y_high[x])
    put_x(xs, 0, x_low, c_low)
    put_x(xs, 5, x_high, c_high)
    for x in range(4):
        masks = window_mask(kept, x)
        for p in range(2):
            keep = both_rows(masks, p)
            la = a_in[p, x]
            ld = xd[p, x + 1, 64:192, :]
            for e in range(-1, 2):
                cols = slice(256 * (e + 1), 256 * (e + 2))
                cubic = dense_product(la, xd, p, x, e) + dense_product(ld, xs, p, x, e)
                linear = s_in[p, x, :, cols].astype(F32)
                total = ((3.0 * linear - 2.0 * cubic) * keep[:, cols]).astype(BF)
                first = slice(192 * (e + 1), 192 * (e + 2))
                out[x, 2 * p, :, first] = total[0:64, 0:192]
                out[x, 2 * p + 1, :, first] = total[64:128, 64:256]


def call(kernel, outs, scratch=()):
    return pl.pallas_call(
        kernel,
        out_shape=[jax.ShapeDtypeStruct(s, BF) for s in outs],
        out_specs=[VMEM] * len(outs),
        scratch_shapes=[pltpu.VMEM(s, BF) for s in scratch],
        compiler_params=pltpu.CompilerParams(vmem_limit_bytes=48 * 1024 * 1024),
    )


def shift(value, axis, step):
    count = lax.axis_size(axis)
    return lax.ppermute(value, axis, [(i, (i + step) % count) for i in range(count)])


def corners(low, high, x):
    return jnp.stack([low[:, x, :, 128:256], high[:, x, :, 128:256]], axis=1)


def exchange(y_up, y_down, x_up, x_down):
    y_low = shift(y_up, "gy", 1)
    y_high = shift(y_down, "gy", -1)
    x_low = shift(x_up, "gx", 1)
    x_high = shift(x_down, "gx", -1)
    c_low = shift(corners(y_low, y_high, 3), "gx", 1)
    c_high = shift(corners(y_low, y_high, 0), "gx", -1)
    return y_low, y_high, x_low, x_high, c_low, c_high


def per_device(ham, dens, pattern, kept):
    ym, xm = (4, W, 384), (6, W, 128)
    msg = call(pack_kernel, [(2,) + ym, (2,) + ym, (2,) + xm, (2,) + xm])(ham, dens, pattern)
    halo = exchange(*msg)
    dense = (2, 6, 256, 768)
    rows = (2, 4, 128, 768)
    a, s, xd, *msg = call(first_kernel, [rows, rows, dense, ym, ym, xm, xm], [dense])(
        ham, dens, pattern, kept, *halo
    )
    halo = exchange(*[m[None] for m in msg])
    return call(last_kernel, [ham.shape], [dense])(a, s, xd, kept, *[h[0] for h in halo])[0]


def solution(mesh):
    return jax.shard_map(
        per_device,
        mesh=mesh,
        in_specs=(
            P("gx", "gy", None, None),
            P("gx", "gy", None, None),
            P("gx", "gy", None),
            P("gx", "gy", None),
        ),
        out_specs=P("gx", "gy", None, None),
        check_vma=False,
    )
```

```python
import jax
import jax.numpy as jnp
from jax import lax
from jax.experimental import pallas as pl
from jax.experimental.pallas import tpu as pltpu
from jax.sharding import PartitionSpec as P

W = 64
BF = jnp.bfloat16
F32 = jnp.float32
VMEM = pl.BlockSpec(memory_space=pltpu.VMEM)


def spot(x, y, x2, y2):
    p = y // 2
    return p, x + 1, W * (y - 2 * p + 1), 256 * (x2 - x + 1) + W * (y2 - 2 * p + 1)


def block(dense, x, y, x2, y2):
    p, i, r, c = spot(x, y, x2, y2)
    return dense[p, i, r : r + W, c : c + W]


def strip_mask(mask_ref, x):
    slot = lax.broadcasted_iota(jnp.int32, (9, 9 * W), 0)
    lane = lax.broadcasted_iota(jnp.int32, (9, 9 * W), 1)
    spread = (lane // W == slot).astype(BF)
    flags = mask_ref[x].astype(F32).astype(BF)
    return jnp.dot(flags, spread, preferred_element_type=F32)


def window_mask(mask_ref, x):
    slot = lax.broadcasted_iota(jnp.int32, (9, 12 * W), 0)
    lane = lax.broadcasted_iota(jnp.int32, (9, 12 * W), 1)
    flags = mask_ref[x].astype(F32).astype(BF)
    out = []
    for r in range(2):
        dy = (lane % 256) // W - r
        inside = (dy >= 0) & (dy <= 2) & (lane // 256 * 3 + dy == slot)
        out.append(jnp.dot(flags, inside.astype(BF), preferred_element_type=F32))
    return out


def both_rows(masks, p):
    first, second = masks
    return jnp.concatenate(
        [
            jnp.broadcast_to(first[2 * p : 2 * p + 1], (W, 768)),
            jnp.broadcast_to(second[2 * p + 1 : 2 * p + 2], (W, 768)),
        ],
        axis=0,
    )


def put_strips(dst, ref, pattern):
    zero = jnp.zeros((W, W), BF)
    for x in range(4):
        mask = strip_mask(pattern, x).astype(BF)
        for y in range(4):
            strip = ref[x, y] * mask[y : y + 1]
            p, r = y // 2, y % 2
            for d in range(3):
                piece = strip[:, 192 * d : 192 * d + 192]
                parts = [piece, zero] if r == 0 else [zero, piece]
                dst[p, x + 1, W + W * r : 2 * W + W * r, 256 * d : 256 * d + 256] = (
                    jnp.concatenate(parts, axis=1)
                )


def put_shared(dst):
    zero = jnp.zeros((W, 128), BF)
    for i in range(1, 5):
        for d in range(3):
            c = 256 * d
            dst[1, i, 0:64, c : c + 128] = dst[0, i, 128:192, c + 128 : c + 256]
            dst[1, i, 0:64, c + 128 : c + 256] = zero
            dst[0, i, 192:256, c + 128 : c + 256] = dst[1, i, 64:128, c : c + 128]
            dst[0, i, 192:256, c : c + 128] = zero


def put_y(dst, side, along=None, across=None):
    zero = jnp.zeros((W, W), BF)
    y, halo = (0, -1) if side == 0 else (3, 4)
    for x in range(4):
        for d in (-1, 0, 1):
            x2 = x + d
            same = zero if along is None else along(x, x2)
            if 0 <= x2 < 4:
                inner = block(dst, x2, y, x, halo).T
            else:
                inner = zero if across is None else across(x, x2)
            rest = jnp.zeros((W, 128), BF)
            parts = [same, inner, rest] if side == 0 else [rest, inner, same]
            c = 256 * (d + 1)
            dst[side, x + 1, 192 * side : 192 * side + W, c : c + 256] = jnp.concatenate(parts, axis=1)


def put_x(dst, side, within=None):
    zero = jnp.zeros((W, W), BF)
    at, edge, out, back = (0, 1, 0, 2) if side == 0 else (5, 4, 2, 0)
    for p in range(2):
        if within is not None:
            first = 2 * p - 1
            rows = [
                jnp.concatenate(
                    [
                        within(first + i, first + j) if abs(i - j) <= 1 else zero
                        for j in range(4)
                    ],
                    axis=1,
                )
                for i in range(4)
            ]
            dst[p, at, :, 256:512] = jnp.concatenate(rows, axis=0)
        else:
            dst[p, at, :, 256:512] = jnp.zeros((256, 256), BF)
        dst[p, at, :, 256 * back : 256 * back + 256] = dst[
            p, edge, :, 256 * out : 256 * out + 256
        ].T


def dense_product(left, right, p, x, e, cols=(0, 256)):
    total = None
    for d in range(max(-1, e - 1), min(1, e + 1) + 1):
        c = 256 * (e - d + 1)
        term = jnp.dot(
            left[:, 256 * (d + 1) : 256 * (d + 2)],
            right[p, x + 1 + d, :, c + cols[0] : c + cols[1]],
            preferred_element_type=F32,
        )
        total = term if total is None else total + term
    return total


def line_message(blocks, ends, flags):
    tiles = []
    for get in blocks:
        tiles += [jnp.concatenate([get(i, i), get(i, i + 1)], axis=1) for i in range(4)]
    tiles.append(jnp.concatenate([blocks[0](0, -1), blocks[1](0, -1)], axis=1))
    rows = [jnp.broadcast_to(f, (16, W)).astype(BF) for f in flags]
    tiles.append(jnp.concatenate([blocks[2](0, -1), jnp.concatenate(rows, axis=0)], axis=1))
    for pair in ends:
        tiles.append(jnp.concatenate(pair, axis=1))
    return tiles


def local_kernel(
    ham, dens, pattern, kept, cy_up, cy_down, y_up, y_down, x_up, x_down, xh, xd, xs
):
    for ref, dst in ((ham, xh), (dens, xd)):
        put_strips(dst, ref, pattern)
        put_shared(dst)
        for side in range(2):
            put_y(dst, side)
        for side in range(2):
            put_x(dst, side)
    flags = {}
    for x in range(4):
        masks = window_mask(kept, x)
        for p in range(2):
            keep = both_rows(masks, p)
            for e in range(-1 if x == 0 else 0, 2):
                cols = slice(256 * (e + 1), 256 * (e + 2))
                whole = x in (0, 3) and e == 0
                rows = slice(64, 192) if whole or x in (0, 3) else slice(64 + W * p, 128 + W * p)
                part = slice(rows.start - 64, rows.stop - 64)
                total = dense_product(xh[p, x + 1, rows, :], xd, p, x, e)
                total += dense_product(xd[p, x + 1, rows, :], xh, p, x, e)
                xs[p, x + 1, rows, cols] = (total * keep[part, cols]).astype(BF)
        flags[x] = strip_mask(kept, x)
    mats = (xh, xd, xs)
    order = (xs, xh, xd)

    def flag(x, y, dx, dy):
        k = 3 * (dx + 1) + dy + 1
        return flags[x][y : y + 1, W * k : W * k + W]

    for x, out, dx in ((3, x_up, 1), (0, x_down, -1)):
        get = [lambda i, j, m=m: block(m, x, i, x, j) for m in mats]
        marks = [flag(x, 0, 0, -1), flag(x, 0, dx, -1), flag(x, 3, 0, 1), flag(x, 3, dx, 1)]
        for n, tile in enumerate(line_message(get, [], marks)):
            out[n] = tile
    for y, out, corner, dy in ((3, y_up, cy_up, 1), (0, y_down, cy_down, -1)):
        get = [lambda i, j, m=m: block(m, i, y, j, y) for m in mats]
        marks = [flag(0, y, -1, 0), flag(0, y, -1, dy), flag(3, y, 1, 0), flag(3, y, 1, dy)]
        ends = [[block(m, x, y, x2, y + dy) for m in (xh, xd)] for x, x2 in ((0, -1), (3, 4))]
        for n, tile in enumerate(line_message(get, ends, marks)):
            out[n] = tile
        for n, (x, x2) in enumerate(((0, -1), (3, 4))):
            parts = [block(m, x, y, x, y) for m in order]
            parts += [block(xs, x, y, x2, y), block(xs, x, y, x, y + dy), jnp.zeros((W, W), BF)]
            corner[n] = jnp.concatenate(parts, axis=1)


def line_blocks(msg, n, corners, first=None, last=None):
    def right(i):
        if i == 3 and last is not None:
            return last
        return msg[4 * n + i][:, W:]

    def left():
        if first is not None:
            return first
        return msg[12][:, W * n : W * n + W]

    def get(i, j):
        if i == j:
            return corners[0 if i < 0 else 1] if i in (-1, 4) else msg[4 * n + i][:, :W]
        if (i, j) == (0, -1):
            return left()
        if (i, j) == (-1, 0):
            return left().T
        return right(i) if j > i else right(j).T

    return get


def last_kernel(
    ham, dens, pattern, kept, y_low, y_high, x_low, x_high, c_low, c_high, out, xh, xd, xs, a_rows
):
    ys, xm, cs = (y_low, y_high), (x_low, x_high), (c_low, c_high)
    def corner(sx, sy, k):
        return cs[sx][sy][:, W * k : W * k + W]

    for n, (ref, dst) in enumerate(((ham, xh), (dens, xd))):
        put_strips(dst, ref, pattern)
        put_shared(dst)
        for side in range(2):
            m = ys[side]
            line = line_blocks(m, n, None)
            put_y(
                dst,
                side,
                line,
                lambda x, x2, m=m, n=n: m[14 if x == 0 else 15][:, W * n : W * n + W],
            )
        for side in range(2):
            put_x(dst, side, line_blocks(xm[side], n, [corner(side, t, n + 1) for t in range(2)]))
    for x in range(4):
        masks = window_mask(kept, x)
        for p in range(2):
            keep = both_rows(masks, p)
            lh = xh[p, x + 1, 64:192, :]
            ld = xd[p, x + 1, 64:192, :]
            for e in range(-1, 2):
                cols = slice(256 * (e + 1), 256 * (e + 2))
                a = dense_product(lh, xd, p, x, e) * keep[:, cols]
                b = dense_product(ld, xh, p, x, e) * keep[:, cols]
                a_rows[p, x, :, cols] = a.astype(BF)
                xs[p, x + 1, 64:192, cols] = (a + b).astype(BF)
    put_shared(xs)
    firsts = {}
    for sx in range(2):
        hx, ex, go, back = (0, 1, 0, 2) if sx == 0 else (5, 4, 2, 0)
        for sy in range(2):
            hp, ep, base = (0, 1, 0) if sy == 0 else (3, 2, 128)

            def at(m, k, f):
                part = 256 * (f[0] - k[0] + 1)
                rows = slice(base, base + 128) if k[1] is None else slice(W * k[1], W * k[1] + W)
                start = part + (base if f[1] is None else W * f[1])
                return m[sy, k[0], rows, start : start + (128 if f[1] is None else W)]

            def through(k, m, f):
                return jnp.dot(
                    at(xh, k, m), at(xd, m, f), preferred_element_type=F32
                ) + jnp.dot(at(xd, k, m), at(xh, m, f), preferred_element_type=F32)

            a, b, c, d = (hx, hp), (hx, ep), (ex, hp), (ex, ep)
            halo, brick = (hx, None), (ex, None)
            xt, yt = xm[sx], ys[sy]
            ba = xt[13][:, :W] if sy == 0 else xt[11][:, W:]
            ca = yt[13][:, :W] if sx == 0 else yt[11][:, W:]
            keep_ba = xt[13][32 * sy : 32 * sy + 1, W:].astype(F32)
            keep_bc = xt[13][32 * sy + 16 : 32 * sy + 17, W:].astype(F32)
            keep_ca = yt[13][32 * sx : 32 * sx + 1, W:].astype(F32)
            s_ba = ba.astype(F32) + corner(sx, sy, 4).astype(F32).T + through(b, brick, a) * keep_ba
            s_ca = (
                ca.astype(F32)
                + corner(sx, sy, 3).astype(F32).T
                + (through(c, b, a) + through(c, d, a)) * keep_ca
            )
            s_bc = (through(b, halo, c) + through(b, brick, c)) * keep_bc
            firsts[sx, sy] = s_ba.astype(BF), s_ca.astype(BF), s_bc.astype(BF).T
    for sy in range(2):
        line = line_blocks(ys[sy], 2, None, firsts[0, sy][1], firsts[1, sy][1])
        put_y(xs, sy, line, lambda x, x2, sy=sy: firsts[0 if x == 0 else 1, sy][2])
    for sx in range(2):
        put_x(
            xs,
            sx,
            line_blocks(
                xm[sx], 2, [corner(sx, t, 0) for t in range(2)], firsts[sx, 0][0], firsts[sx, 1][0]
            ),
        )
    for x in range(4):
        masks = window_mask(kept, x)
        for p in range(2):
            keep = both_rows(masks, p)
            la = a_rows[p, x]
            ld = xd[p, x + 1, 64:192, :]
            for e in range(-1, 2):
                cols = slice(256 * (e + 1), 256 * (e + 2))
                cubic = dense_product(la, xd, p, x, e) + dense_product(ld, xs, p, x, e)
                linear = xs[p, x + 1, 64:192, cols].astype(F32)
                total = ((3.0 * linear - 2.0 * cubic) * keep[:, cols]).astype(BF)
                first = slice(192 * (e + 1), 192 * (e + 2))
                out[x, 2 * p, :, first] = total[0:64, 0:192]
                out[x, 2 * p + 1, :, first] = total[64:128, 64:256]


def call(kernel, outs, scratch=()):
    return pl.pallas_call(
        kernel,
        out_shape=[jax.ShapeDtypeStruct(s, BF) for s in outs],
        out_specs=[VMEM] * len(outs),
        scratch_shapes=[pltpu.VMEM(s, BF) for s in scratch],
        compiler_params=pltpu.CompilerParams(vmem_limit_bytes=48 * 1024 * 1024),
    )


def shift(value, axis, step):
    count = lax.axis_size(axis)
    return lax.ppermute(value, axis, [(i, (i + step) % count) for i in range(count)])


def per_device(ham, dens, pattern, kept):
    dense = (2, 6, 256, 768)
    corner, y_line, x_line = (2, W, 384), (16, W, 128), (14, W, 128)
    cy_up, cy_down, y_up, y_down, x_up, x_down = call(
        local_kernel, [corner, corner, y_line, y_line, x_line, x_line], [dense] * 3
    )(ham, dens, pattern, kept)
    cy_low = shift(cy_up, "gy", 1)
    cy_high = shift(cy_down, "gy", -1)
    x_low = shift(x_up, "gx", 1)
    y_low = shift(y_up, "gy", 1)
    y_high = shift(y_down, "gy", -1)
    x_high = shift(x_down, "gx", -1)
    c_low = shift(jnp.stack([cy_low[1], cy_high[1]]), "gx", 1)
    c_high = shift(jnp.stack([cy_low[0], cy_high[0]]), "gx", -1)
    return call(last_kernel, [ham.shape], [dense] * 3 + [(2, 4, 128, 768)])(
        ham, dens, pattern, kept, y_low, y_high, x_low, x_high, c_low, c_high
    )[0]


def solution(mesh):
    return jax.shard_map(
        per_device,
        mesh=mesh,
        in_specs=(
            P("gx", "gy", None, None),
            P("gx", "gy", None, None),
            P("gx", "gy", None),
            P("gx", "gy", None),
        ),
        out_specs=P("gx", "gy", None, None),
        check_vma=False,
    )
```

```python
import jax
import jax.numpy as jnp
from jax import lax
from jax.experimental import pallas as pl
from jax.experimental.pallas import tpu as pltpu
from jax.sharding import PartitionSpec as P

W = 64
BF = jnp.bfloat16
F32 = jnp.float32
VMEM = pl.BlockSpec(memory_space=pltpu.VMEM)


def spot(x, y, x2, y2):
    p = y // 2
    return p, x + 1, W * (y - 2 * p + 1), 256 * (x2 - x + 1) + W * (y2 - 2 * p + 1)


def block(dense, x, y, x2, y2):
    p, i, r, c = spot(x, y, x2, y2)
    return dense[p, i, r : r + W, c : c + W]


def strip_mask(mask_ref, x):
    slot = lax.broadcasted_iota(jnp.int32, (9, 9 * W), 0)
    lane = lax.broadcasted_iota(jnp.int32, (9, 9 * W), 1)
    spread = (lane // W == slot).astype(BF)
    flags = mask_ref[x].astype(F32).astype(BF)
    return jnp.dot(flags, spread, preferred_element_type=F32)


def window_mask(mask_ref, x):
    slot = lax.broadcasted_iota(jnp.int32, (9, 12 * W), 0)
    lane = lax.broadcasted_iota(jnp.int32, (9, 12 * W), 1)
    flags = mask_ref[x].astype(F32).astype(BF)
    out = []
    for r in range(2):
        dy = (lane % 256) // W - r
        inside = (dy >= 0) & (dy <= 2) & (lane // 256 * 3 + dy == slot)
        out.append(jnp.dot(flags, inside.astype(BF), preferred_element_type=F32))
    return out


def both_rows(wide, x, p):
    return jnp.concatenate(
        [
            jnp.broadcast_to(wide[x, 0, 2 * p : 2 * p + 1, :], (W, 768)),
            jnp.broadcast_to(wide[x, 1, 2 * p + 1 : 2 * p + 2, :], (W, 768)),
        ],
        axis=0,
    )


def put_strips(dst, ref):
    zero = jnp.zeros((W, W), BF)
    for x in range(4):
        for y in range(4):
            strip = ref[x, y]
            p, r = y // 2, y % 2
            for d in range(3):
                piece = strip[:, 192 * d : 192 * d + 192]
                parts = [piece, zero] if r == 0 else [zero, piece]
                dst[p, x + 1, W + W * r : 2 * W + W * r, 256 * d : 256 * d + 256] = (
                    jnp.concatenate(parts, axis=1)
                )


def put_shared(dst):
    zero = jnp.zeros((W, 128), BF)
    for i in range(1, 5):
        for d in range(3):
            c = 256 * d
            dst[1, i, 0:64, c : c + 128] = dst[0, i, 128:192, c + 128 : c + 256]
            dst[1, i, 0:64, c + 128 : c + 256] = zero
            dst[0, i, 192:256, c + 128 : c + 256] = dst[1, i, 64:128, c : c + 128]
            dst[0, i, 192:256, c : c + 128] = zero


def put_y(dst, side, along=None, across=None):
    zero = jnp.zeros((W, W), BF)
    y, halo = (0, -1) if side == 0 else (3, 4)
    for x in range(4):
        for d in (-1, 0, 1):
            x2 = x + d
            same = zero if along is None else along(x, x2)
            if 0 <= x2 < 4:
                inner = block(dst, x2, y, x, halo).T
            else:
                inner = zero if across is None else across(x, x2)
            rest = jnp.zeros((W, 128), BF)
            parts = [same, inner, rest] if side == 0 else [rest, inner, same]
            c = 256 * (d + 1)
            dst[side, x + 1, 192 * side : 192 * side + W, c : c + 256] = jnp.concatenate(parts, axis=1)


def put_x(dst, side, within=None):
    zero = jnp.zeros((W, W), BF)
    at, edge, out, back = (0, 1, 0, 2) if side == 0 else (5, 4, 2, 0)
    for p in range(2):
        if within is not None:
            first = 2 * p - 1
            rows = [
                jnp.concatenate(
                    [
                        within(first + i, first + j) if abs(i - j) <= 1 else zero
                        for j in range(4)
                    ],
                    axis=1,
                )
                for i in range(4)
            ]
            dst[p, at, :, 256:512] = jnp.concatenate(rows, axis=0)
        else:
            dst[p, at, :, 256:512] = jnp.zeros((256, 256), BF)
        dst[p, at, :, 256 * back : 256 * back + 256] = dst[
            p, edge, :, 256 * out : 256 * out + 256
        ].T


def dense_product(left, right, p, x, e, cols=(0, 256)):
    total = None
    for d in range(max(-1, e - 1), min(1, e + 1) + 1):
        c = 256 * (e - d + 1)
        term = jnp.dot(
            left[:, 256 * (d + 1) : 256 * (d + 2)],
            right[p, x + 1 + d, :, c + cols[0] : c + cols[1]],
            preferred_element_type=F32,
        )
        total = term if total is None else total + term
    return total


def line_message(blocks, ends, flags):
    tiles = []
    for get in blocks:
        tiles += [jnp.concatenate([get(i, i), get(i, i + 1)], axis=1) for i in range(4)]
    tiles.append(jnp.concatenate([blocks[0](0, -1), blocks[1](0, -1)], axis=1))
    rows = [jnp.broadcast_to(f, (16, W)).astype(BF) for f in flags]
    tiles.append(jnp.concatenate([blocks[2](0, -1), jnp.concatenate(rows, axis=0)], axis=1))
    for pair in ends:
        tiles.append(jnp.concatenate(pair, axis=1))
    return tiles


def send_kernel(
    ham, dens, pattern, kept, cy_up, cy_down, ends, y_up, y_down, x_up, x_down, hm, dm, wide,
    hb, db, pb, kb, live, keep, sems, mask_sems,
):
    masks = [
        pltpu.make_async_copy(pattern, pb, mask_sems.at[0]),
        pltpu.make_async_copy(kept, kb, mask_sems.at[1]),
    ]
    copies = []
    for x in (0, 3, 1, 2):
        for n, (ref, buf) in enumerate(((ham, hb), (dens, db))):
            copies.append(pltpu.make_async_copy(ref.at[x], buf.at[x], sems.at[n, x]))
    for copy in masks + copies:
        copy.start()
    for copy in masks:
        copy.wait()
    for x in range(4):
        live[x] = strip_mask(pb, x)
        keep[x] = strip_mask(kb, x)
        wide[x, 0], wide[x, 1] = window_mask(kb, x)
    for copy in copies:
        copy.wait()
    for x in range(4):
        for y in range(4):
            mask = live[x, y : y + 1, :].astype(BF)
            hm[x, y] = hb[x, y] * mask
            dm[x, y] = db[x, y] * mask

    def lanes(dx, dy):
        k = 3 * (dx + 1) + dy + 1
        return slice(W * k, W * k + W)

    def flag(x, y, dx, dy):
        return keep[x, y : y + 1, lanes(dx, dy)]

    def get(ref, x, y, dx, dy):
        return ref[x, y, :, lanes(dx, dy)]

    def through(x, y, cells, dx, dy):
        left, right = [], []
        for first, second in ((hm, dm), (dm, hm)):
            for mx, my in cells:
                left.append(get(first, x, y, mx - x, my - y))
                right.append(get(second, mx, my, x + dx - mx, y + dy - my))
        total = jnp.dot(
            jnp.concatenate(left, axis=1), jnp.concatenate(right, axis=0), preferred_element_type=F32
        )
        return (total * flag(x, y, dx, dy)).astype(BF)

    def rows(left, right):
        return lax.dot_general(left, right, (((1,), (1,)), ((), ())), preferred_element_type=F32)

    def own(x, y):
        total = rows(hm[x, y], dm[x, y])
        return ((total + total.T) * flag(x, y, 0, 0)).astype(BF)

    def link(x, y, dx, dy):
        if dx == 1:
            parts = [(slice(192, 576), slice(0, 384))]
        else:
            parts = [(slice(192 * d + 64, 192 * d + 192), slice(192 * d, 192 * d + 128)) for d in range(3)]
        left, right = [], []
        for first, second in ((hm, dm), (dm, hm)):
            left += [first[x, y, :, one] for one, _ in parts]
            right += [second[x + dx, y + dy, :, other] for _, other in parts]
        total = rows(jnp.concatenate(left, axis=1), jnp.concatenate(right, axis=1))
        return (total * flag(x, y, dx, dy)).astype(BF)

    def pair(one, two):
        return jnp.concatenate([one, two], axis=1)

    selfs = {(x, y): own(x, y) for x in range(4) for y in range(4) if x in (0, 3) or y in (0, 3)}
    for y, out, dy in ((3, cy_up, 1), (0, cy_down, -1)):
        for n, (x, dx) in enumerate(((0, -1), (3, 1))):
            across = through(x, y, ((x, y), (x - dx, y)), 0, dy)
            out[n, 0] = pair(selfs[x, y], get(hm, x, y, 0, 0))
            out[n, 1] = pair(get(dm, x, y, 0, 0), through(x, y, ((x, y), (x, y - dy)), dx, 0))
            out[n, 2] = pair(across, jnp.zeros((W, W), BF))
            ends[0 if y == 0 else 1, n] = across.T

    def line(out, cell, step, marks):
        dx, dy = step
        for i in range(4):
            x, y = cell(i)
            for n, ref in enumerate((hm, dm)):
                out[4 * n + i] = pair(get(ref, x, y, 0, 0), get(ref, x, y, dx, dy))
            if i < 3:
                out[9 + i] = pair(selfs[x, y], link(x, y, dx, dy))
            else:
                rows = [jnp.broadcast_to(m, (16, W)).astype(BF) for m in marks]
                out[12] = pair(selfs[x, y], jnp.concatenate(rows, axis=0))
        x, y = cell(0)
        out[8] = pair(get(hm, x, y, -dx, -dy), get(dm, x, y, -dx, -dy))

    for x, out, dx in ((3, x_up, 1), (0, x_down, -1)):
        marks = [flag(x, 0, 0, -1), flag(x, 0, dx, -1), flag(x, 3, 0, 1), flag(x, 3, dx, 1)]
        line(out, lambda i: (x, i), (0, 1), marks)
    for y, out, dy in ((3, y_up, 1), (0, y_down, -1)):
        marks = [flag(0, y, -1, 0), flag(0, y, -1, dy), flag(3, y, 1, 0), flag(3, y, 1, dy)]
        line(out, lambda i: (i, y), (1, 0), marks)
        for n, (x, dx) in enumerate(((0, -1), (3, 1))):
            out[13 + n] = pair(get(hm, x, y, dx, dy), get(dm, x, y, dx, dy))


def line_blocks(msg, n, corners, first=None, last=None):
    base = 4 * n if n < 2 else 9

    def right(i):
        if i == 3 and last is not None:
            return last
        return msg[base + i][:, W:]

    def left():
        if first is not None:
            return first
        return msg[8][:, W * n : W * n + W]

    def get(i, j):
        if i == j:
            return corners[0 if i < 0 else 1] if i in (-1, 4) else msg[base + i][:, :W]
        if (i, j) == (0, -1):
            return left()
        if (i, j) == (-1, 0):
            return left().T
        return right(i) if j > i else right(j).T

    return get


def last_kernel(
    ham, dens, wide, y_low, y_high, x_low, x_high, cy_low, cy_high, c_low, c_high,
    out, xh, xd, xs, a_rows,
):
    ys, xm, cys, cs = (y_low, y_high), (x_low, x_high), (cy_low, cy_high), (c_low, c_high)

    def corner(sx, sy, k):
        if k == 4:
            return cs[sx][4][:, W * sy : W * sy + W]
        return cs[sx][2 * sy + k // 2][:, W * (k % 2) : W * (k % 2) + W]

    for n, (ref, dst) in enumerate(((ham, xh), (dens, xd))):
        put_strips(dst, ref)
        put_shared(dst)
        for side in range(2):
            m = ys[side]
            line = line_blocks(m, n, None)
            put_y(
                dst,
                side,
                line,
                lambda x, x2, m=m, n=n: m[13 if x == 0 else 14][:, W * n : W * n + W],
            )
        for side in range(2):
            put_x(dst, side, line_blocks(xm[side], n, [corner(side, t, n + 1) for t in range(2)]))
    for x in range(4):
        for p in range(2):
            mask = both_rows(wide, x, p)
            lh = xh[p, x + 1, 64:192, :]
            ld = xd[p, x + 1, 64:192, :]
            for e in range(-1, 2):
                cols = slice(256 * (e + 1), 256 * (e + 2))
                a = dense_product(lh, xd, p, x, e) * mask[:, cols]
                b = dense_product(ld, xh, p, x, e) * mask[:, cols]
                a_rows[p, x, :, cols] = a.astype(BF)
                xs[p, x + 1, 64:192, cols] = (a + b).astype(BF)
    put_shared(xs)
    firsts = {}
    for sx in range(2):
        hx, ex, go, back = (0, 1, 0, 2) if sx == 0 else (5, 4, 2, 0)
        for sy in range(2):
            hp, ep, base = (0, 1, 0) if sy == 0 else (3, 2, 128)

            def at(m, k, f):
                part = 256 * (f[0] - k[0] + 1)
                rows = slice(base, base + 128) if k[1] is None else slice(W * k[1], W * k[1] + W)
                start = part + (base if f[1] is None else W * f[1])
                return m[sy, k[0], rows, start : start + (128 if f[1] is None else W)]

            def through(k, m, f):
                return jnp.dot(
                    at(xh, k, m), at(xd, m, f), preferred_element_type=F32
                ) + jnp.dot(at(xd, k, m), at(xh, m, f), preferred_element_type=F32)

            a, b, c, d = (hx, hp), (hx, ep), (ex, hp), (ex, ep)
            halo, brick = (hx, None), (ex, None)
            xt, yt = xm[sx], ys[sy]
            ca = cys[sy][sx, 1][:, W:]
            keep_ba = xt[12][32 * sy : 32 * sy + 1, W:].astype(F32)
            keep_bc = xt[12][32 * sy + 16 : 32 * sy + 17, W:].astype(F32)
            keep_ca = yt[12][32 * sx : 32 * sx + 1, W:].astype(F32)
            s_ba = corner(sx, sy, 4).astype(F32).T + through(b, brick, a) * keep_ba
            s_ca = (
                ca.astype(F32)
                + corner(sx, sy, 3).astype(F32).T
                + (through(c, b, a) + through(c, d, a)) * keep_ca
            )
            s_bc = (through(b, halo, c) + through(b, brick, c)) * keep_bc
            firsts[sx, sy] = s_ba.astype(BF), s_ca.astype(BF), s_bc.astype(BF).T
    for sy in range(2):
        line = line_blocks(ys[sy], 2, None, firsts[0, sy][1], firsts[1, sy][1])
        put_y(xs, sy, line, lambda x, x2, sy=sy: firsts[0 if x == 0 else 1, sy][2])
    for sx in range(2):
        put_x(
            xs,
            sx,
            line_blocks(
                xm[sx], 2, [corner(sx, t, 0) for t in range(2)], firsts[sx, 0][0], firsts[sx, 1][0]
            ),
        )
    for x in range(4):
        for p in range(2):
            mask = both_rows(wide, x, p)
            la = a_rows[p, x]
            ld = xd[p, x + 1, 64:192, :]
            for e in range(-1, 2):
                cols = slice(256 * (e + 1), 256 * (e + 2))
                cubic = dense_product(la, xd, p, x, e) + dense_product(ld, xs, p, x, e)
                linear = xs[p, x + 1, 64:192, cols].astype(F32)
                total = ((3.0 * linear - 2.0 * cubic) * mask[:, cols]).astype(BF)
                first = slice(192 * (e + 1), 192 * (e + 2))
                out[x, 2 * p, :, first] = total[0:64, 0:192]
                out[x, 2 * p + 1, :, first] = total[64:128, 64:256]


def call(kernel, outs, scratch=(), inputs=pl.no_block_spec, limit=48):
    def shape(s):
        return s if isinstance(s, jax.ShapeDtypeStruct) else jax.ShapeDtypeStruct(s, BF)

    return pl.pallas_call(
        kernel,
        out_shape=[shape(s) for s in outs],
        in_specs=inputs,
        out_specs=[VMEM] * len(outs),
        scratch_shapes=[pltpu.VMEM(s, BF) if isinstance(s, tuple) else s for s in scratch],
        compiler_params=pltpu.CompilerParams(vmem_limit_bytes=limit * 1024 * 1024),
    )


def shift(value, axis, step):
    count = lax.axis_size(axis)
    return lax.ppermute(value, axis, [(i, (i + step) % count) for i in range(count)])


def per_device(ham, dens, pattern, kept):
    dense = (2, 6, 256, 768)
    corner, y_line, x_line = (2, 3, W, 128), (15, W, 128), (13, W, 128)
    mask = pltpu.VMEM(pattern.shape, pattern.dtype)
    flags = pltpu.VMEM((4, 4, 9 * W), F32)
    inputs = [pltpu.with_memory_space_constraint(v, pltpu.HBM) for v in (ham, dens, pattern, kept)]
    cy_up, cy_down, ends, y_up, y_down, x_up, x_down, ham, dens, wide = call(
        send_kernel,
        [corner, corner, (2, 2, W, W), y_line, y_line, x_line, x_line, ham.shape, dens.shape]
        + [jax.ShapeDtypeStruct((4, 2, 4, 12 * W), F32)],
        [ham.shape, dens.shape, mask, mask, flags, flags]
        + [pltpu.SemaphoreType.DMA((2, 4)), pltpu.SemaphoreType.DMA((2,))],
        [pl.BlockSpec(memory_space=pl.ANY)] * 4,
        16,
    )(*inputs)
    cy_low = shift(cy_up, "gy", 1)
    cy_high = shift(cy_down, "gy", -1)
    x_high = shift(x_down, "gx", -1)
    x_low = shift(x_up, "gx", 1)
    y_low = shift(y_up, "gy", 1)
    y_down, y_low = lax.optimization_barrier((y_down, y_low))
    y_high = shift(y_down, "gy", -1)

    def forward(n):
        sums = [v[n, 2, :, :W] + ends[s, n] for s, v in enumerate((cy_low, cy_high))]
        return jnp.concatenate([cy_low[n, :2], cy_high[n, :2], jnp.concatenate(sums, axis=1)[None]])

    c_high = shift(forward(0), "gx", -1)
    c_low = shift(forward(1), "gx", 1)
    return call(last_kernel, [ham.shape], [dense] * 3 + [(2, 4, 128, 768)])(
        ham, dens, wide, y_low, y_high, x_low, x_high, cy_low, cy_high, c_low, c_high
    )[0]


def solution(mesh):
    return jax.shard_map(
        per_device,
        mesh=mesh,
        in_specs=(
            P("gx", "gy", None, None),
            P("gx", "gy", None, None),
            P("gx", "gy", None),
            P("gx", "gy", None),
        ),
        out_specs=P("gx", "gy", None, None),
        check_vma=False,
    )
```

```python
import jax
import jax.numpy as jnp
from jax import lax
from jax.experimental import pallas as pl
from jax.experimental.pallas import tpu as pltpu
from jax.sharding import PartitionSpec as P

W = 64
BF = jnp.bfloat16
F32 = jnp.float32
VMEM = pl.BlockSpec(memory_space=pltpu.VMEM)


def spot(x, y, x2, y2):
    p = y // 2
    return p, x + 1, W * (y - 2 * p + 1), 256 * (x2 - x + 1) + W * (y2 - 2 * p + 1)


def block(dense, x, y, x2, y2):
    p, i, r, c = spot(x, y, x2, y2)
    return dense[p, i, r : r + W, c : c + W]


def strip_mask(mask_ref, x):
    slot = lax.broadcasted_iota(jnp.int32, (9, 9 * W), 0)
    lane = lax.broadcasted_iota(jnp.int32, (9, 9 * W), 1)
    spread = (lane // W == slot).astype(BF)
    flags = mask_ref[x].astype(F32).astype(BF)
    return jnp.dot(flags, spread, preferred_element_type=F32)


def window_mask(mask_ref, x):
    slot = lax.broadcasted_iota(jnp.int32, (9, 12 * W), 0)
    lane = lax.broadcasted_iota(jnp.int32, (9, 12 * W), 1)
    flags = mask_ref[x].astype(F32).astype(BF)
    out = []
    for r in range(2):
        dy = (lane % 256) // W - r
        inside = (dy >= 0) & (dy <= 2) & (lane // 256 * 3 + dy == slot)
        out.append(jnp.dot(flags, inside.astype(BF), preferred_element_type=F32))
    return out


def both_rows(wide, x, p):
    return jnp.concatenate(
        [
            jnp.broadcast_to(wide[x, 0, 2 * p : 2 * p + 1, :], (W, 768)),
            jnp.broadcast_to(wide[x, 1, 2 * p + 1 : 2 * p + 2, :], (W, 768)),
        ],
        axis=0,
    )


def put_strips(dst, ref):
    zero = jnp.zeros((W, W), BF)
    for x in range(4):
        for y in range(4):
            strip = ref[x, y]
            p, r = y // 2, y % 2
            for d in range(3):
                piece = strip[:, 192 * d : 192 * d + 192]
                parts = [piece, zero] if r == 0 else [zero, piece]
                dst[p, x + 1, W + W * r : 2 * W + W * r, 256 * d : 256 * d + 256] = (
                    jnp.concatenate(parts, axis=1)
                )


def put_shared(dst):
    zero = jnp.zeros((W, 128), BF)
    for i in range(1, 5):
        for d in range(3):
            c = 256 * d
            dst[1, i, 0:64, c : c + 128] = dst[0, i, 128:192, c + 128 : c + 256]
            dst[1, i, 0:64, c + 128 : c + 256] = zero
            dst[0, i, 192:256, c + 128 : c + 256] = dst[1, i, 64:128, c : c + 128]
            dst[0, i, 192:256, c : c + 128] = zero


def put_y(dst, side, along, across=None):
    zero = jnp.zeros((W, W), BF)
    y, halo = (0, -1) if side == 0 else (3, 4)
    for x in range(4):
        for d in (-1, 0, 1):
            x2 = x + d
            inside = 0 <= x2 < 4
            if not inside and across is None:
                continue
            same = along(x, x2)
            inner = block(dst, x2, y, x, halo).T if inside else across(x, x2)
            rest = jnp.zeros((W, 128), BF)
            parts = [same, inner, rest] if side == 0 else [rest, inner, same]
            c = 256 * (d + 1)
            dst[side, x + 1, 192 * side : 192 * side + W, c : c + 256] = jnp.concatenate(parts, axis=1)


def lower_blocks(places):
    row = lax.broadcasted_iota(jnp.int32, (256, 256), 0) // W
    col = lax.broadcasted_iota(jnp.int32, (256, 256), 1) // W
    hit = None
    for i, j in places:
        here = (row == i) & (col == j)
        hit = here if hit is None else hit | here
    return hit.astype(BF)


def dense_product(left, right, p, x, e, brick=False):
    total = None
    for d in range(max(-1, e - 1), min(1, e + 1) + 1):
        if brick and not 0 <= x + d < 4:
            continue
        term = jnp.dot(
            left[:, 256 * (d + 1) : 256 * (d + 2)],
            right[p, x + 1 + d, :, 256 * (e - d + 1) : 256 * (e - d + 2)],
            preferred_element_type=F32,
        )
        total = term if total is None else total + term
    return total


def line_message(blocks, ends, flags):
    tiles = []
    for get in blocks:
        tiles += [jnp.concatenate([get(i, i), get(i, i + 1)], axis=1) for i in range(4)]
    tiles.append(jnp.concatenate([blocks[0](0, -1), blocks[1](0, -1)], axis=1))
    rows = [jnp.broadcast_to(f, (16, W)).astype(BF) for f in flags]
    tiles.append(jnp.concatenate([blocks[2](0, -1), jnp.concatenate(rows, axis=0)], axis=1))
    for pair in ends:
        tiles.append(jnp.concatenate(pair, axis=1))
    return tiles


def send_kernel(
    ham, dens, pattern, kept, ends, cy_up, cy_down, y_up, y_down, x_up, x_down, hm, dm, wide,
    hb, db, pb, kb, live, keep, sems, mask_sems,
):
    masks = [
        pltpu.make_async_copy(pattern, pb, mask_sems.at[0]),
        pltpu.make_async_copy(kept, kb, mask_sems.at[1]),
    ]
    copies = []
    for x in (0, 3, 1, 2):
        for n, (ref, buf) in enumerate(((ham, hb), (dens, db))):
            copies.append(pltpu.make_async_copy(ref.at[x], buf.at[x], sems.at[n, x]))
    for copy in masks + copies:
        copy.start()
    for copy in masks:
        copy.wait()
    for x in range(4):
        live[x] = strip_mask(pb, x)
        keep[x] = strip_mask(kb, x)
        wide[x, 0], wide[x, 1] = window_mask(kb, x)
    for copy in copies:
        copy.wait()
    for x in range(4):
        for y in range(4):
            mask = live[x, y : y + 1, :].astype(BF)
            hm[x, y] = hb[x, y] * mask
            dm[x, y] = db[x, y] * mask

    def lanes(dx, dy):
        k = 3 * (dx + 1) + dy + 1
        return slice(W * k, W * k + W)

    def flag(x, y, dx, dy):
        return keep[x, y : y + 1, lanes(dx, dy)]

    def get(ref, x, y, dx, dy):
        return ref[x, y, :, lanes(dx, dy)]

    def through(x, y, cells, dx, dy):
        left, right = [], []
        for first, second in ((hm, dm), (dm, hm)):
            for mx, my in cells:
                left.append(get(first, x, y, mx - x, my - y))
                right.append(get(second, mx, my, x + dx - mx, y + dy - my))
        total = jnp.dot(
            jnp.concatenate(left, axis=1), jnp.concatenate(right, axis=0), preferred_element_type=F32
        )
        return (total * flag(x, y, dx, dy)).astype(BF)

    def rows(left, right):
        return lax.dot_general(left, right, (((1,), (1,)), ((), ())), preferred_element_type=F32)

    def own(x, y):
        total = rows(hm[x, y], dm[x, y])
        return ((total + total.T) * flag(x, y, 0, 0)).astype(BF)

    def link(x, y, dx, dy):
        if dx == 1:
            parts = [(slice(192, 576), slice(0, 384))]
        else:
            parts = [(slice(192 * d + 64, 192 * d + 192), slice(192 * d, 192 * d + 128)) for d in range(3)]
        left, right = [], []
        for first, second in ((hm, dm), (dm, hm)):
            left += [first[x, y, :, one] for one, _ in parts]
            right += [second[x + dx, y + dy, :, other] for _, other in parts]
        total = rows(jnp.concatenate(left, axis=1), jnp.concatenate(right, axis=1))
        return (total * flag(x, y, dx, dy)).astype(BF)

    def pair(one, two):
        return jnp.concatenate([one, two], axis=1)

    selfs = {(x, y): own(x, y) for x in range(4) for y in range(4) if x in (0, 3) or y in (0, 3)}
    for y, out, dy in ((3, cy_up, 1), (0, cy_down, -1)):
        for n, (x, dx) in enumerate(((0, -1), (3, 1))):
            across = through(x, y, ((x - dx, y),), 0, dy)
            along = through(x, y, ((x, y - dy),), dx, 0)
            out[3 * n] = pair(selfs[x, y], get(hm, x, y, 0, 0))
            out[3 * n + 1] = pair(get(dm, x, y, 0, 0), along)
            out[3 * n + 2] = pair(across, along.T)
            ends[0 if y == 0 else 1, n] = across.T

    def line(out, cell, step, marks):
        dx, dy = step
        for i in range(4):
            x, y = cell(i)
            for n, ref in enumerate((hm, dm)):
                out[4 * n + i] = pair(get(ref, x, y, 0, 0), get(ref, x, y, dx, dy))
            if i < 3:
                out[9 + i] = pair(selfs[x, y], link(x, y, dx, dy))
            else:
                rows = [jnp.broadcast_to(m, (16, W)).astype(BF) for m in marks]
                out[12] = pair(selfs[x, y], jnp.concatenate(rows, axis=0))
        x, y = cell(0)
        out[8] = pair(get(hm, x, y, -dx, -dy), get(dm, x, y, -dx, -dy))

    for x, out, dx in ((3, x_up, 1), (0, x_down, -1)):
        marks = [flag(x, 0, 0, -1), flag(x, 0, dx, -1), flag(x, 3, 0, 1), flag(x, 3, dx, 1)]
        line(out, lambda i: (x, i), (0, 1), marks)
    for y, out, dy in ((3, y_up, 1), (0, y_down, -1)):
        marks = [flag(0, y, -1, 0), flag(0, y, -1, dy), flag(3, y, 1, 0), flag(3, y, 1, dy)]
        line(out, lambda i: (i, y), (1, 0), marks)
        for n, (x, dx) in enumerate(((0, -1), (3, 1))):
            out[13 + n] = pair(get(hm, x, y, dx, dy), get(dm, x, y, dx, dy))


def line_blocks(msg, n, corners, first=None, last=None):
    base = 4 * n if n < 2 else 9

    def right(i):
        if i == 3 and last is not None:
            return last
        return msg[base + i][:, W:]

    def left():
        if first is not None:
            return first
        return msg[8][:, W * n : W * n + W]

    def get(i, j):
        if i == j:
            return corners[0 if i < 0 else 1] if i in (-1, 4) else msg[base + i][:, :W]
        if (i, j) == (0, -1):
            return left()
        if (i, j) == (-1, 0):
            return left().T
        return right(i) if j > i else right(j).T

    return get


def edge(side):
    return (0, 0, 1, 2) if side == 0 else (3, 2, 1, 0)


def part(n):
    return slice(256 * n, 256 * n + 256)


def unpack_rows(total, p, x, e, out):
    cols = slice(192 * (e + 1), 192 * (e + 2))
    out[x, 2 * p, :, cols] = total[0:64, 0:192]
    out[x, 2 * p + 1, :, cols] = total[64:128, 64:256]


def middle_kernel(
    ham, dens, wide, y_low, y_high, out, h_edge, d_edge, h_back, d_back, a_edge, g_edge, done_edge,
    xh, xd, xs, a_rows, rows, sems,
):
    ys = (y_low, y_high)
    for n, (ref, dst, keep, turned) in enumerate(
        ((ham, xh, h_edge, h_back), (dens, xd, d_edge, d_back))
    ):
        put_strips(dst, ref)
        put_shared(dst)
        for side in range(2):
            m = ys[side]
            put_y(
                dst,
                side,
                line_blocks(m, n, None),
                lambda x, x2, m=m, n=n: m[13 if x == 0 else 14][:, W * n : W * n + W],
            )
        for side in range(2):
            x, go, _, back = edge(side)
            for p in range(2):
                tile = dst[p, x + 1, :, part(go)].T
                dst[p, 5 * side, :, part(back)] = tile
                turned[side, p] = tile
                keep[side, p] = dst[p, x + 1]
    for x in range(4):
        for p in range(2):
            mask = both_rows(wide, x, p)
            lh = xh[p, x + 1, 64:192, :]
            ld = xd[p, x + 1, 64:192, :]
            for e in range(-1, 2):
                if 0 <= x + e < 4:
                    cols = part(e + 1)
                    a = dense_product(lh, xd, p, x, e) * mask[:, cols]
                    b = dense_product(ld, xh, p, x, e) * mask[:, cols]
                    a_rows[p, x, :, cols] = a.astype(BF)
                    xs[p, x + 1, 64:192, cols] = (a + b).astype(BF)
    put_shared(xs)
    for side in range(2):
        put_y(xs, side, line_blocks(ys[side], 2, None))
        for p in range(2):
            x = edge(side)[0]
            a_edge[side, p] = a_rows[p, x, :, part(1)]
    for x in (1, 2, 0, 3):
        for p in range(2):
            mask = both_rows(wide, x, p)
            la = a_rows[p, x]
            ld = xd[p, x + 1, 64:192, :]
            for e in range(-1, 2):
                if not 0 <= x + e < 4:
                    continue
                cols = part(e + 1)
                cubic = dense_product(la, xd, p, x, e, True) + dense_product(ld, xs, p, x, e, True)
                total = 3.0 * xs[p, x + 1, 64:192, cols].astype(F32) - 2.0 * cubic
                if x in (1, 2):
                    unpack_rows((total * mask[:, cols]).astype(BF), p, x - 1, e, rows)
                elif e == 0:
                    g_edge[x // 3, p] = total
                else:
                    done_edge[x // 3, p] = (total * mask[:, cols]).astype(BF)
        if x == 2:
            copy = pltpu.make_async_copy(rows, out.at[1:3], sems.at[0])
            copy.start()
    copy.wait()


def last_kernel(
    wide, y_low, y_high, cy_low, cy_high, x_low, x_high, c_low, h_edge, d_edge, h_back, d_back, a_edge, g_edge,
    done_edge, given, out, hh, dh, sh, ss, sb, u, a_go, rows, sems,
):
    ys, cys, xm, cs = (y_low, y_high), (cy_low, cy_high), (x_low, x_high), (c_low, x_high.at[13:18])
    both = [(sx, p) for sx in range(2) for p in range(2)]

    def corner(sx, sy, k):
        if k == 4:
            return cs[sx][4][:, W * sy : W * sy + W]
        return cs[sx][2 * sy + k // 2][:, W * (k % 2) : W * (k % 2) + W]

    def dot(left, right):
        return jnp.dot(left, right, preferred_element_type=F32)

    def fill(dst, sx, n, corners, crossing):
        msg, base = xm[sx], 4 * n if n < 2 else 9
        for p in range(2):
            u[sx, p, :, :] = jnp.zeros((256, 256), BF)
            for i in range(4):
                y = 2 * p - 1 + i
                at = slice(W * i, W * i + W)
                if y in (-1, 4):
                    u[sx, p, at, at] = corners[p]
                    continue
                whole = i < 3 and not (n == 2 and y == 3)
                u[sx, p, at, W * i : W * i + W * (2 if whole else 1)] = (
                    msg[base + y] if whole else msg[base + y][:, :W]
                )
            places = crossing(u, p)
            tile = u[sx, p]
            dst[sx, p] = tile + tile.T * lower_blocks(places)

    def crossing_of(sx, n):
        def put(u, p):
            if p == 1:
                return ((1, 0), (2, 1), (3, 2))
            u[sx, 0, 64:128, 0:64] = xm[sx][8][:, W * n : W * n + W]
            return ((0, 1), (2, 1), (3, 2))

        return put

    for sx in range(2):
        for n, halo in enumerate((hh, dh)):
            fill(halo, sx, n, [corner(sx, t, n + 1) for t in range(2)], crossing_of(sx, n))
    for sx, p in both:
        x, go, _, back = edge(sx)
        mask = both_rows(wide, x, p)[:, part(go)]

        def to_halo(left, right, halo):
            left = left[sx, p, 64:192, :]
            return dot(left[:, part(go)], halo[sx, p]) + dot(
                left[:, part(1)], right[sx, p, :, part(go)]
            )

        a = to_halo(h_edge, d_edge, dh) * mask
        b = to_halo(d_edge, h_edge, hh) * mask
        a_go[sx, p] = a.astype(BF)
        ss[sx, p, 64:192, :] = (a + b).astype(BF)
    z2 = jnp.zeros((W, 128), BF)
    ab = {}
    for sx, sy in both:
        x, go, _, back = edge(sx)
        two = slice(128 * sy, 128 * sy + 128)
        hp, ep = (0, 1) if sy == 0 else (1, 0)

        def four(row, halo, back_tile):
            def cols(n):
                return slice(256 * n + 128 * sy, 256 * n + 128 * sy + 128)

            top = [halo[sx, sy, two, two], back_tile[sx, sy, two, two]]
            low = [row[sx, sy, two, cols(go)], row[sx, sy, two, cols(1)]]
            return jnp.concatenate(
                [jnp.concatenate(top, axis=1), jnp.concatenate(low, axis=1)], axis=0
            )

        qh, qd = four(h_edge, hh, h_back), four(d_edge, dh, d_back)
        q = dot(jnp.concatenate([qh, qd], axis=1), jnp.concatenate([qd, qh], axis=0))

        def blk(i, j):
            return q[W * i : W * i + W, W * j : W * j + W]

        a, b, c = hp, ep, 2 + hp
        xt, yt = xm[sx], ys[sy]
        keep_ba = xt[12][32 * sy : 32 * sy + 1, W:].astype(F32)
        keep_bc = xt[12][32 * sy + 16 : 32 * sy + 17, W:].astype(F32)
        keep_ca = yt[12][32 * sx : 32 * sx + 1, W:].astype(F32)
        ab[sx, sy] = (corner(sx, sy, 4).astype(F32) + keep_ba * blk(a, b)).astype(BF)
        ca = cys[sy][1 + 3 * sx][:, W:].astype(F32) + corner(sx, sy, 3).astype(F32) + keep_ca * blk(c, a)
        ca, cb = ca.astype(BF), (keep_bc * blk(c, b)).astype(BF)
        here = slice(192 * sy, 192 * sy + W)
        ss[sx, sy, here, :] = jnp.concatenate([ca, cb, z2] if sy == 0 else [z2, cb, ca], axis=1)
    for sx in range(2):
        ss[sx, 1, 0:64, :] = jnp.concatenate([ss[sx, 0, 128:192, 128:256], z2], axis=1)
        ss[sx, 0, 192:256, :] = jnp.concatenate([z2, ss[sx, 1, 64:128, 0:128]], axis=1)

        def put(u, p, sx=sx):
            if p == 0:
                u[sx, 0, 0:64, 64:128] = ab[sx, 0]
                return ((1, 0), (2, 1), (3, 2))
            u[sx, 1, 192:256, 128:192] = ab[sx, 1]
            return ((1, 0), (2, 1), (2, 3))

        fill(sh, sx, 2, [corner(sx, t, 0) for t in range(2)], put)
        for p in range(2):
            sb[sx, p] = ss[sx, p].T
    copies = []
    for sx, p in both:
        x, go, _, back = edge(sx)
        mask = both_rows(wide, x, p)
        ld = d_edge[sx, p, 64:192, :]
        outer = dot(a_go[sx, p], dh[sx, p]) + dot(ld[:, part(go)], sh[sx, p])
        outer += dot(a_edge[sx, p], d_edge[sx, p, :, part(go)]) + dot(ld[:, part(1)], ss[sx, p])
        outer = 3.0 * ss[sx, p, 64:192, :].astype(F32) - 2.0 * outer
        same = dot(a_go[sx, p], d_back[sx, p]) + dot(ld[:, part(go)], sb[sx, p])
        same = g_edge[sx, p] - 2.0 * same
        unpack_rows((outer * mask[:, part(go)]).astype(BF), p, sx, go - 1, rows)
        unpack_rows((same * mask[:, part(1)]).astype(BF), p, sx, 0, rows)
        unpack_rows(done_edge[sx, p], p, sx, back - 1, rows)
        if p == 1:
            copies.append(pltpu.make_async_copy(rows.at[sx], out.at[x], sems.at[sx]))
            copies[-1].start()
    for copy in copies:
        copy.wait()


ANY = pl.BlockSpec(memory_space=pl.ANY)


def call(kernel, outs, scratch, inputs, limit, spaces=None, aliases=None):
    def shape(s):
        return s if isinstance(s, jax.ShapeDtypeStruct) else jax.ShapeDtypeStruct(s, BF)

    return pl.pallas_call(
        kernel,
        out_shape=[shape(s) for s in outs],
        in_specs=inputs,
        out_specs=spaces or [VMEM] * len(outs),
        scratch_shapes=[pltpu.VMEM(s, BF) if isinstance(s, tuple) else s for s in scratch],
        input_output_aliases=aliases or {},
        compiler_params=pltpu.CompilerParams(vmem_limit_bytes=limit * 1024 * 1024),
    )


def shift(value, axis, step):
    count = lax.axis_size(axis)
    return lax.ppermute(value, axis, [(i, (i + step) % count) for i in range(count)])


def per_device(ham, dens, pattern, kept):
    dense = (2, 6, 256, 768)
    corner, y_line, x_line = (6, W, 128), (15, W, 128), (13, W, 128)
    mask = pltpu.VMEM(pattern.shape, pattern.dtype)
    flags = pltpu.VMEM((4, 4, 9 * W), F32)
    inputs = [pltpu.with_memory_space_constraint(v, pltpu.HBM) for v in (ham, dens, pattern, kept)]
    ends, cy_up, cy_down, y_up, y_down, x_up, x_down, ham, dens, wide = call(
        send_kernel,
        [(2, 2, W, W), corner, corner, y_line, y_line, x_line, x_line, ham.shape, dens.shape]
        + [jax.ShapeDtypeStruct((4, 2, 4, 12 * W), F32)],
        [ham.shape, dens.shape, mask, mask, flags, flags]
        + [pltpu.SemaphoreType.DMA((2, 4)), pltpu.SemaphoreType.DMA((2,))],
        [ANY] * 4,
        16,
    )(*inputs)
    cy_low = shift(cy_up, "gy", 1)
    cy_high = shift(cy_down, "gy", -1)
    y_low = shift(y_up, "gy", 1)
    y_high = shift(y_down, "gy", -1)
    x_low = shift(x_up, "gx", 1)

    def forward(n):
        at = 3 * n
        tiles = []
        for v in (cy_low, cy_high):
            tiles += [v[at], jnp.concatenate([v[at + 1, :, :W], v[at + 2, :, W:]], axis=1)]
        sums = [v[at + 2, :, :W] + ends[s, n] for s, v in enumerate((cy_low, cy_high))]
        return jnp.stack(tiles + [jnp.concatenate(sums, axis=1)])

    x_high = shift(jnp.concatenate([x_down, forward(0)]), "gx", -1)
    c_low = shift(forward(1), "gx", 1)
    edges = [(2, 2, 256, 768)] * 2 + [(2, 2, 256, 256)] * 2 + [(2, 2, 128, 256)]
    edges += [jax.ShapeDtypeStruct((2, 2, 128, 256), F32), (2, 2, 128, 256)]
    out, *edges = call(
        middle_kernel,
        [ham.shape] + edges,
        [dense] * 3 + [(2, 4, 128, 768), (2, 4, W, 9 * W), pltpu.SemaphoreType.DMA((1,))],
        [VMEM] * 5,
        32,
        [ANY] + [VMEM] * 7,
    )(ham, dens, wide, y_low, y_high)
    tile, rows = (2, 2, 256, 256), (2, 4, W, 9 * W)
    return call(
        last_kernel,
        [ham.shape],
        [tile] * 6 + [(2, 2, 128, 256), rows, pltpu.SemaphoreType.DMA((2,))],
        [VMEM] * 15 + [ANY],
        32,
        [ANY],
        {15: 0},
    )(wide, y_low, y_high, cy_low, cy_high, x_low, x_high, c_low, *edges, out)[0]


def solution(mesh):
    return jax.shard_map(
        per_device,
        mesh=mesh,
        in_specs=(
            P("gx", "gy", None, None),
            P("gx", "gy", None, None),
            P("gx", "gy", None),
            P("gx", "gy", None),
        ),
        out_specs=P("gx", "gy", None, None),
        check_vma=False,
    )
```

```python
import jax
import jax.numpy as jnp
from jax import lax
from jax.experimental import pallas as pl
from jax.experimental.pallas import tpu as pltpu
from jax.sharding import PartitionSpec as P

W = 64
BF = jnp.bfloat16
F32 = jnp.float32
VMEM = pl.BlockSpec(memory_space=pltpu.VMEM)


def spot(x, y, x2, y2):
    p = y // 2
    return p, x + 1, W * (y - 2 * p + 1), 256 * (x2 - x + 1) + W * (y2 - 2 * p + 1)


def block(dense, x, y, x2, y2):
    p, i, r, c = spot(x, y, x2, y2)
    return dense[p, i, r : r + W, c : c + W]


def triangles():
    row = lax.broadcasted_iota(jnp.int32, (W, W), 0)
    col = lax.broadcasted_iota(jnp.int32, (W, W), 1)
    return [m.astype(F32).astype(BF) for m in (row <= col, row > col, row == col)]


def strip_mask(mask_ref, x):
    slot = lax.broadcasted_iota(jnp.int32, (9, 9 * W), 0)
    lane = lax.broadcasted_iota(jnp.int32, (9, 9 * W), 1)
    spread = (lane // W == slot).astype(BF)
    flags = mask_ref[x].astype(F32).astype(BF)
    return jnp.dot(flags, spread, preferred_element_type=F32)


def window_mask(mask_ref, x):
    slot = lax.broadcasted_iota(jnp.int32, (9, 12 * W), 0)
    lane = lax.broadcasted_iota(jnp.int32, (9, 12 * W), 1)
    flags = mask_ref[x].astype(F32).astype(BF)
    out = []
    for r in range(2):
        dy = (lane % 256) // W - r
        inside = (dy >= 0) & (dy <= 2) & (lane // 256 * 3 + dy == slot)
        out.append(jnp.dot(flags, inside.astype(BF), preferred_element_type=F32))
    return out


def both_rows(wide, x, p):
    return jnp.concatenate(
        [
            jnp.broadcast_to(wide[x, 0, 2 * p : 2 * p + 1, :], (W, 768)),
            jnp.broadcast_to(wide[x, 1, 2 * p + 1 : 2 * p + 2, :], (W, 768)),
        ],
        axis=0,
    )


def put_strips(dst, ref):
    zero = jnp.zeros((W, W), BF)
    for x in range(4):
        for y in range(4):
            strip = ref[x, y]
            p, r = y // 2, y % 2
            for d in range(3):
                piece = strip[:, 192 * d : 192 * d + 192]
                parts = [piece, zero] if r == 0 else [zero, piece]
                dst[p, x + 1, W + W * r : 2 * W + W * r, 256 * d : 256 * d + 256] = (
                    jnp.concatenate(parts, axis=1)
                )


def put_shared(dst):
    zero = jnp.zeros((W, 128), BF)
    for i in range(1, 5):
        for d in range(3):
            c = 256 * d
            dst[1, i, 0:64, c : c + 128] = dst[0, i, 128:192, c + 128 : c + 256]
            dst[1, i, 0:64, c + 128 : c + 256] = zero
            dst[0, i, 192:256, c + 128 : c + 256] = dst[1, i, 64:128, c : c + 128]
            dst[0, i, 192:256, c : c + 128] = zero


def put_y(dst, side, msg, n, masks, add):
    y, halo = (0, -1) if side == 0 else (3, 4)
    same, after, before = line_tiles([line_cell(msg, n, i, 0, masks) for i in range(4)])

    def along(x, x2):
        c, d = x // 2, x2 // 2
        tile = same[c] if c == d else after[0] if c < d else before[0]
        return tile[W * (x % 2) : W * (x % 2) + W, W * (x2 % 2) : W * (x2 % 2) + W]

    for x in range(4):
        for x2 in range(max(0, x - 1), min(3, x + 1) + 1):
            add[W * x : W * x + W, W * x2 : W * x2 + W] = block(dst, x, y, x2, halo)
    inner = add[...].T
    rest = jnp.zeros((W, 128), BF)
    for x in range(4):
        for d in (-1, 0, 1):
            x2 = x + d
            if 0 <= x2 < 4:
                two = along(x, x2), inner[W * x : W * x + W, W * x2 : W * x2 + W]
            elif n == 2:
                continue
            elif x == 0:
                link = msg[6][:, W * n : W * n + W]
                two = link, msg[10][:, W * n : W * n + W]
            else:
                two = msg[3 if n == 0 else 5][:, :W], msg[11][:, W * n : W * n + W]
            parts = [*two, rest] if side == 0 else [rest, two[1], two[0]]
            c = 256 * (d + 1)
            dst[side, x + 1, 192 * side : 192 * side + W, c : c + 256] = jnp.concatenate(parts, axis=1)


def dense_product(left, right, p, x, e, brick=False):
    total = None
    for d in range(max(-1, e - 1), min(1, e + 1) + 1):
        if brick and not 0 <= x + d < 4:
            continue
        term = jnp.dot(
            left[:, 256 * (d + 1) : 256 * (d + 2)],
            right[p, x + 1 + d, :, 256 * (e - d + 1) : 256 * (e - d + 2)],
            preferred_element_type=F32,
        )
        total = term if total is None else total + term
    return total


def line_message(blocks, ends, flags):
    tiles = []
    for get in blocks:
        tiles += [jnp.concatenate([get(i, i), get(i, i + 1)], axis=1) for i in range(4)]
    tiles.append(jnp.concatenate([blocks[0](0, -1), blocks[1](0, -1)], axis=1))
    rows = [jnp.broadcast_to(f, (16, W)).astype(BF) for f in flags]
    tiles.append(jnp.concatenate([blocks[2](0, -1), jnp.concatenate(rows, axis=0)], axis=1))
    for pair in ends:
        tiles.append(jnp.concatenate(pair, axis=1))
    return tiles


def send_kernel(
    ham, dens, pattern, kept, ends_up, ends_down, cy_up, cy_down, y_up, y_down, x_up, x_down, hm, dm, wide,
    hb, db, pb, kb, live, keep, sems, mask_sems,
):
    masks = [
        pltpu.make_async_copy(pattern, pb, mask_sems.at[0]),
        pltpu.make_async_copy(kept, kb, mask_sems.at[1]),
    ]
    copies = {x: [] for x in (0, 3, 1, 2)}
    for x in copies:
        for n, (ref, buf) in enumerate(((ham, hb), (dens, db))):
            copies[x].append(pltpu.make_async_copy(ref.at[x], buf.at[x], sems.at[n, x]))
    for copy in masks + sum(copies.values(), []):
        copy.start()
    for copy in masks:
        copy.wait()
    for x in range(4):
        live[x] = strip_mask(pb, x)
        keep[x] = strip_mask(kb, x)

    def arrive(x):
        for copy in copies[x]:
            copy.wait()
        for y in range(4):
            mask = live[x, y : y + 1, :].astype(BF)
            hm[x, y] = hb[x, y] * mask
            dm[x, y] = db[x, y] * mask

    def lanes(dx, dy):
        k = 3 * (dx + 1) + dy + 1
        return slice(W * k, W * k + W)

    def flag(x, y, dx, dy):
        return keep[x, y : y + 1, lanes(dx, dy)]

    def get(ref, x, y, dx, dy):
        return ref[x, y, :, lanes(dx, dy)]

    def through(x, y, cells, dx, dy):
        left, right = [], []
        for first, second in ((hm, dm), (dm, hm)):
            for mx, my in cells:
                left.append(get(first, x, y, mx - x, my - y))
                right.append(get(second, mx, my, x + dx - mx, y + dy - my))
        total = jnp.dot(
            jnp.concatenate(left, axis=1), jnp.concatenate(right, axis=0), preferred_element_type=F32
        )
        return (total * flag(x, y, dx, dy)).astype(BF)

    def rows(left, right):
        return lax.dot_general(left, right, (((1,), (1,)), ((), ())), preferred_element_type=F32)

    def own(x, y):
        total = rows(hm[x, y], dm[x, y]) + rows(dm[x, y], hm[x, y])
        return (total * flag(x, y, 0, 0)).astype(BF)

    def link(x, y, dx, dy):
        if dx == 1:
            parts = [(slice(192, 576), slice(0, 384))]
        else:
            parts = [(slice(192 * d + 64, 192 * d + 192), slice(192 * d, 192 * d + 128)) for d in range(3)]
        left, right = [], []
        for first, second in ((hm, dm), (dm, hm)):
            left += [first[x, y, :, one] for one, _ in parts]
            right += [second[x + dx, y + dy, :, other] for _, other in parts]
        total = rows(jnp.concatenate(left, axis=1), jnp.concatenate(right, axis=1))
        return (total * flag(x, y, dx, dy)).astype(BF)

    def pair(one, two, swap=0):
        return jnp.concatenate([two, one] if swap else [one, two], axis=1)

    upper, lower, eye = triangles()
    selfs = {}

    def packed(x, y):
        return get(hm, x, y, 0, 0) * upper + get(dm, x, y, 0, 0) * lower

    def diagonal(value):
        return jnp.sum((value * eye).astype(F32), axis=0, keepdims=True)

    row = lax.broadcasted_iota(jnp.int32, (W, W), 0)
    col = lax.broadcasted_iota(jnp.int32, (W, W), 1)
    def put_line(out, cell, step, marks, first):
        dx, dy = step
        cells = [cell(i) for i in range(4)]
        items = list(marks)
        for i, (x, y) in enumerate(cells):
            out[i] = pair(packed(x, y), get(hm, x, y, dx, dy), (first + i) % 2)
            items.append(diagonal(get(dm, x, y, 0, 0)))
        items += [diagonal(selfs[cells[i]]) for i in (2, 3)]
        even = 1 - first % 2
        for i in range(2):
            one, two = cells[2 * i], cells[2 * i + 1]
            out[4 + i] = pair(get(dm, *one, dx, dy), get(dm, *two, dx, dy), even)
        x, y = cells[0]
        out[6] = pair(get(hm, x, y, -dx, -dy), get(dm, x, y, -dx, -dy))
        mixed = [selfs[cells[i]] * upper + selfs[cells[i + 2]] * lower for i in range(2)]
        out[7] = pair(*mixed, 1 - even)
        out[8] = pair(link(*cells[0], dx, dy), link(*cells[1], dx, dy), even)
        rows = jnp.zeros((16, W), F32)
        for k, item in enumerate(items):
            rows = jnp.where(row[:16] == k, item, rows)
        rows = jnp.concatenate([rows.astype(BF), jnp.zeros((48, W), BF)], axis=0)
        out[9] = pair(link(*cells[2], dx, dy), rows, even)

    arrive(0)
    arrive(3)
    for x, out, dx in ((0, x_down, -1), (3, x_up, 1)):
        selfs.update({(x, y): own(x, y) for y in range(4)})
        marks = [flag(x, 0, 0, -1), flag(x, 0, dx, -1), flag(x, 3, 0, 1), flag(x, 3, dx, 1)]
        put_line(out, lambda i: (x, i), (0, 1), marks, 1)
    arrive(1)
    arrive(2)
    for x in (1, 2):
        selfs.update({(x, y): own(x, y) for y in (0, 3)})
    ends_up[...] = jnp.zeros_like(ends_up)
    ends_down[...] = jnp.zeros_like(ends_down)
    for y, out, line, dy in ((3, cy_up, y_up, 1), (0, cy_down, y_down, -1)):
        alongs = []
        for n, (x, dx) in enumerate(((0, -1), (3, 1))):
            across = through(x, y, ((x - dx, y),), 0, dy)
            along = through(x, y, ((x, y - dy),), dx, 0)
            alongs.append(along)
            low = diagonal(get(dm, x, y, 0, 0))
            low = jnp.where(row == col + 1, low, jnp.where((row == 63) & (col == 0), low[:, 63:64], 0.0))
            odd = 1 if y == 0 else 0
            out[2 * n] = pair(selfs[x, y] * upper + low.astype(BF), across, odd)
            out[2 * n + 1] = pair(packed(x, y), along.T, odd)
            ends = ends_up if x == 3 else ends_down
            if y == 0:
                ends[0, :, W:] = across.T
            else:
                ends[2, :, 0:W] = across.T
        line[12] = pair(*alongs)

    for y, out, dy in ((3, y_up, 1), (0, y_down, -1)):
        marks = [flag(0, y, -1, 0), flag(0, y, -1, dy), flag(3, y, 1, 0), flag(3, y, 1, dy)]
        put_line(out, lambda i: (i, y), (1, 0), marks, 0)
        for n, (x, dx) in enumerate(((0, -1), (3, 1))):
            out[10 + n] = pair(get(hm, x, y, dx, dy), get(dm, x, y, dx, dy))
    for x in range(4):
        wide[x, 0], wide[x, 1] = window_mask(kb, x)


def halves(odd):
    row = lax.broadcasted_iota(jnp.int32, (W, 128), 0)
    col = lax.broadcasted_iota(jnp.int32, (W, 128), 1) - W * odd
    mine = (col >= 0) & (col < W)
    masks = (mine & (row <= col), mine & (row > col), mine & (row == col), jnp.logical_not(mine))
    return [m.astype(F32).astype(BF) for m in masks]


def line_cell(msg, n, i, first, masks):
    odd = (first + i) % 2
    upper, lower, eye, other = masks[odd]
    own = msg[i] if n < 2 else msg[7]
    if n == 0:
        link = own * other
    else:
        link = None if n == 2 and i == 3 else msg[4 + 4 * (n - 1) + i // 2] * other
    if n == 1 or n == 2 and i >= 2:
        add = own * lower
        k = 4 + i if n == 1 else 6 + i
        diag = msg[9][k : k + 1, W * (first % 2) : W * (first % 2) + W]
        lay = add + jnp.concatenate([diag, diag], axis=1) * eye
    else:
        lay, add = own * upper, own * (upper - eye)
    if odd or link is None:
        return lay, add, link
    return lay + link, add + link, None


def line_tiles(rows):
    zero = jnp.zeros((W, 128), BF)
    same, after, before = [], [], []
    for c in range(len(rows) // 2):
        one, two = rows[2 * c], rows[2 * c + 1]
        lay = jnp.concatenate([one[0], two[0]], axis=0)
        same.append(lay + jnp.concatenate([one[1], two[1]], axis=0).T)
        if 2 * c + 2 < len(rows):
            after.append(jnp.concatenate([zero, two[2]], axis=0))
            before.append(after[-1].T)
    return same, after, before


def edge(side):
    return (0, 0, 1, 2) if side == 0 else (3, 2, 1, 0)


def part(n):
    return slice(256 * n, 256 * n + 256)


def unpack_rows(total, p, x, e, out):
    cols = slice(192 * (e + 1), 192 * (e + 2))
    out[x, 2 * p, :, cols] = total[0:64, 0:192]
    out[x, 2 * p + 1, :, cols] = total[64:128, 64:256]


def middle_kernel(
    ham, dens, wide, y_low, y_high, out, h_edge, d_edge, h_back, d_back, a_edge, g_edge, done_edge,
    xh, xd, xs, a_rows, rows, add, sems,
):
    ys = (y_low, y_high)
    masks = halves(0), halves(1)
    for n, (ref, dst, keep, turned) in enumerate(
        ((ham, xh, h_edge, h_back), (dens, xd, d_edge, d_back))
    ):
        put_strips(dst, ref)
        put_shared(dst)
        for side in range(2):
            put_y(dst, side, ys[side], n, masks, add.at[2 * side + n])
        for side in range(2):
            x, go, _, back = edge(side)
            for p in range(2):
                tile = dst[p, x + 1, :, part(go)].T
                dst[p, 5 * side, :, part(back)] = tile
                turned[side, p] = tile
                keep[side, p] = dst[p, x + 1]
    for x in range(4):
        for p in range(2):
            mask = both_rows(wide, x, p)
            lh = xh[p, x + 1, 64:192, :]
            ld = xd[p, x + 1, 64:192, :]
            for e in range(-1, 2):
                if 0 <= x + e < 4:
                    cols = part(e + 1)
                    a = dense_product(lh, xd, p, x, e) * mask[:, cols]
                    b = dense_product(ld, xh, p, x, e) * mask[:, cols]
                    a_rows[p, x, :, cols] = a.astype(BF)
                    xs[p, x + 1, 64:192, cols] = (a + b).astype(BF)
    put_shared(xs)
    for side in range(2):
        put_y(xs, side, ys[side], 2, masks, add.at[4 + side])
        for p in range(2):
            x = edge(side)[0]
            a_edge[side, p] = a_rows[p, x, :, part(1)]
    for x in (1, 2, 0, 3):
        for p in range(2):
            mask = both_rows(wide, x, p)
            la = a_rows[p, x]
            ld = xd[p, x + 1, 64:192, :]
            for e in range(-1, 2):
                if not 0 <= x + e < 4:
                    continue
                cols = part(e + 1)
                cubic = dense_product(la, xd, p, x, e, True) + dense_product(ld, xs, p, x, e, True)
                total = 3.0 * xs[p, x + 1, 64:192, cols].astype(F32) - 2.0 * cubic
                if x in (1, 2):
                    unpack_rows((total * mask[:, cols]).astype(BF), p, x - 1, e, rows)
                elif e == 0:
                    g_edge[x // 3, p] = total
                else:
                    done_edge[x // 3, p] = (total * mask[:, cols]).astype(BF)
        if x == 2:
            copy = pltpu.make_async_copy(rows, out.at[1:3], sems.at[0])
            copy.start()
    copy.wait()


def last_kernel(
    wide, y_low, y_high, x_low, x_high, c_low, h_edge, d_edge, h_back, d_back, a_edge, g_edge,
    done_edge, given, out, hh, dh, sh, ss, sb, a_go, rows, sems,
):
    ys, xm, cs = (y_low, y_high), (x_low, x_high), (c_low, x_high.at[10:14])
    both = [(sx, p) for sx in range(2) for p in range(2)]

    masks = halves(0), halves(1)

    def corner_cell(sx, sy, n):
        upper, lower, eye, _ = masks[sy]
        one = cs[sx][2 * sy]
        if n == 2:
            return one * upper, one * (upper - eye), None
        value = cs[sx][2 * sy + 1]
        if n == 0:
            return value * upper, value * (upper - eye), None
        row = lax.broadcasted_iota(jnp.int32, (W, W), 0)
        col = lax.broadcasted_iota(jnp.int32, (W, W), 1)
        spread = one[:, W * sy : W * sy + W].astype(F32)
        low = jnp.sum(jnp.where(row == col + 1, spread, 0.0), axis=0, keepdims=True)
        low += jnp.where(col[0:1] == 63, spread[63:64, 0:1], 0.0)
        below = value * lower
        return below + jnp.concatenate([low, low], axis=1).astype(BF) * eye, below, None

    def tile(ref, sx, p):
        return ref[sx, 128 * p : 128 * p + 256, 128 * p : 128 * p + 256]

    def dot(left, right):
        return jnp.dot(left, right, preferred_element_type=F32)

    def fill(dst, sx, n, crossing):
        rows = [line_cell(xm[sx], n, i, 1, masks) for i in range(4)]
        rows = [corner_cell(sx, 0, n), *rows, corner_cell(sx, 1, n)]
        for place, value in crossing:
            lay, add, rest = rows[place]
            rows[place] = lay + value, add + value, rest
        same, after, before = line_tiles(rows)
        for c in range(3):
            at, to = slice(128 * c, 128 * c + 128), slice(128 * c + 128, 128 * c + 256)
            dst[sx, at, at] = same[c]
            if c < 2:
                dst[sx, at, to] = after[c]
                dst[sx, to, at] = before[c]

    for sx in range(2):
        cross = xm[sx][6]
        fill(hh, sx, 0, [(1, cross * masks[1][3])])
        fill(dh, sx, 1, [(1, jnp.concatenate([cross[:, W:], jnp.zeros((W, W), BF)], axis=1))])
    for sx, p in both:
        x, go, _, back = edge(sx)
        mask = both_rows(wide, x, p)[:, part(go)]

        def to_halo(left, right, halo):
            left = left[sx, p, 64:192, :]
            return dot(left[:, part(go)], tile(halo, sx, p)) + dot(
                left[:, part(1)], right[sx, p, :, part(go)]
            )

        a = to_halo(h_edge, d_edge, dh) * mask
        b = to_halo(d_edge, h_edge, hh) * mask
        a_go[sx, p] = a.astype(BF)
        ss[sx, p, 64:192, :] = (a + b).astype(BF)
    z2 = jnp.zeros((W, 128), BF)
    ab = {}
    for sx, sy in both:
        x, go, _, back = edge(sx)
        two = slice(128 * sy, 128 * sy + 128)
        hp, ep = (0, 1) if sy == 0 else (1, 0)

        def four(row, halo, back_tile):
            def cols(n):
                return slice(256 * n + 128 * sy, 256 * n + 128 * sy + 128)

            top = [tile(halo, sx, sy)[two, two], back_tile[sx, sy, two, two]]
            low = [row[sx, sy, two, cols(go)], row[sx, sy, two, cols(1)]]
            return jnp.concatenate(
                [jnp.concatenate(top, axis=1), jnp.concatenate(low, axis=1)], axis=0
            )

        qh, qd = four(h_edge, hh, h_back), four(d_edge, dh, d_back)
        q = dot(jnp.concatenate([qh, qd], axis=1), jnp.concatenate([qd, qh], axis=0))

        def blk(i, j):
            return q[W * i : W * i + W, W * j : W * j + W]

        a, b, c = hp, ep, 2 + hp
        xt, yt = xm[sx], ys[sy]
        keep_ba = xt[9][2 * sy : 2 * sy + 1, W:].astype(F32)
        keep_bc = xt[9][2 * sy + 1 : 2 * sy + 2, W:].astype(F32)
        keep_ca = yt[9][2 * sx : 2 * sx + 1, :W].astype(F32)
        rest = slice(W * (1 - sy), W * (1 - sy) + W)
        given_ab, given_ca = cs[sx][2 * sy][:, rest], cs[sx][2 * sy + 1][:, rest]
        ab[sx, sy] = (given_ab.astype(F32) + keep_ba * blk(a, b)).astype(BF)
        ca = yt[12][:, W * sx : W * sx + W].astype(F32) + given_ca.astype(F32) + keep_ca * blk(c, a)
        ca, cb = ca.astype(BF), (keep_bc * blk(c, b)).astype(BF)
        here = slice(192 * sy, 192 * sy + W)
        ss[sx, sy, here, :] = jnp.concatenate([ca, cb, z2] if sy == 0 else [z2, cb, ca], axis=1)
    for sx in range(2):
        ss[sx, 1, 0:64, :] = jnp.concatenate([ss[sx, 0, 128:192, 128:256], z2], axis=1)
        ss[sx, 0, 192:256, :] = jnp.concatenate([z2, ss[sx, 1, 64:128, 0:128]], axis=1)

        none = jnp.zeros((W, W), BF)
        crossing = [
            (0, jnp.concatenate([none, ab[sx, 0]], axis=1)),
            (5, jnp.concatenate([ab[sx, 1], none], axis=1)),
        ]
        fill(sh, sx, 2, crossing)
        for p in range(2):
            sb[sx, p] = ss[sx, p].T
    copies = []
    for sx, p in both:
        x, go, _, back = edge(sx)
        mask = both_rows(wide, x, p)
        ld = d_edge[sx, p, 64:192, :]
        outer = dot(a_go[sx, p], tile(dh, sx, p)) + dot(ld[:, part(go)], tile(sh, sx, p))
        outer += dot(a_edge[sx, p], d_edge[sx, p, :, part(go)]) + dot(ld[:, part(1)], ss[sx, p])
        outer = 3.0 * ss[sx, p, 64:192, :].astype(F32) - 2.0 * outer
        same = dot(a_go[sx, p], d_back[sx, p]) + dot(ld[:, part(go)], sb[sx, p])
        same = g_edge[sx, p] - 2.0 * same
        unpack_rows((outer * mask[:, part(go)]).astype(BF), p, sx, go - 1, rows)
        unpack_rows((same * mask[:, part(1)]).astype(BF), p, sx, 0, rows)
        unpack_rows(done_edge[sx, p], p, sx, back - 1, rows)
        if p == 1:
            copies.append(pltpu.make_async_copy(rows.at[sx], out.at[x], sems.at[sx]))
            copies[-1].start()
    for copy in copies:
        copy.wait()


ANY = pl.BlockSpec(memory_space=pl.ANY)


def call(kernel, outs, scratch, inputs, limit, spaces=None, aliases=None):
    def shape(s):
        return s if isinstance(s, jax.ShapeDtypeStruct) else jax.ShapeDtypeStruct(s, BF)

    return pl.pallas_call(
        kernel,
        out_shape=[shape(s) for s in outs],
        in_specs=inputs,
        out_specs=spaces or [VMEM] * len(outs),
        scratch_shapes=[pltpu.VMEM(s, BF) if isinstance(s, tuple) else s for s in scratch],
        input_output_aliases=aliases or {},
        compiler_params=pltpu.CompilerParams(vmem_limit_bytes=limit * 1024 * 1024),
    )


def shift(value, axis, step):
    count = lax.axis_size(axis)
    return lax.ppermute(value, axis, [(i, (i + step) % count) for i in range(count)])


def per_device(ham, dens, pattern, kept):
    dense = (2, 6, 256, 768)
    corner, y_line, x_line = (4, W, 128), (13, W, 128), (10, W, 128)
    mask = pltpu.VMEM(pattern.shape, pattern.dtype)
    flags = pltpu.VMEM((4, 4, 9 * W), F32)
    inputs = [pltpu.with_memory_space_constraint(v, pltpu.HBM) for v in (ham, dens, pattern, kept)]
    ends_up, ends_down, cy_up, cy_down, y_up, y_down, x_up, x_down, ham, dens, wide = call(
        send_kernel,
        [corner] * 4 + [y_line, y_line, x_line, x_line, ham.shape, dens.shape]
        + [jax.ShapeDtypeStruct((4, 2, 4, 12 * W), F32)],
        [ham.shape, dens.shape, mask, mask, flags, flags]
        + [pltpu.SemaphoreType.DMA((2, 4)), pltpu.SemaphoreType.DMA((2,))],
        [ANY] * 4,
        16,
    )(*inputs)
    cy_low = shift(cy_up, "gy", 1)
    cy_high = shift(cy_down, "gy", -1)
    y_low = shift(y_up, "gy", 1)
    y_high = shift(y_down, "gy", -1)
    x_low = shift(x_up, "gx", 1)

    def forward(n, ends):
        at = slice(2 * n, 2 * n + 2)
        return jnp.concatenate([cy_low[at], cy_high[at]]) + ends

    x_high = shift(jnp.concatenate([x_down, forward(0, ends_down)]), "gx", -1)
    c_low = shift(forward(1, ends_up), "gx", 1)
    edges = [(2, 2, 256, 768)] * 2 + [(2, 2, 256, 256)] * 2 + [(2, 2, 128, 256)]
    edges += [jax.ShapeDtypeStruct((2, 2, 128, 256), F32), (2, 2, 128, 256)]
    out, *edges = call(
        middle_kernel,
        [ham.shape] + edges,
        [dense] * 3 + [(2, 4, 128, 768), (2, 4, W, 9 * W)]
        + [(6, 256, 256)]
        + [pltpu.SemaphoreType.DMA((1,))],
        [VMEM] * 5,
        32,
        [ANY] + [VMEM] * 7,
    )(ham, dens, wide, y_low, y_high)
    six, tile, rows = (2, 384, 384), (2, 2, 256, 256), (2, 4, W, 9 * W)
    return call(
        last_kernel,
        [ham.shape],
        [six] * 3
        + [tile] * 2
        + [(2, 2, 128, 256), rows, pltpu.SemaphoreType.DMA((2,))],
        [VMEM] * 13 + [ANY],
        32,
        [ANY],
        {13: 0},
    )(wide, y_low, y_high, x_low, x_high, c_low, *edges, out)[0]


def solution(mesh):
    return jax.shard_map(
        per_device,
        mesh=mesh,
        in_specs=(
            P("gx", "gy", None, None),
            P("gx", "gy", None, None),
            P("gx", "gy", None),
            P("gx", "gy", None),
        ),
        out_specs=P("gx", "gy", None, None),
        check_vma=False,
    )
```

```python
import jax
import jax.numpy as jnp
from jax import lax
from jax.experimental import pallas as pl
from jax.experimental.pallas import tpu as pltpu
from jax.sharding import PartitionSpec as P

W = 64
BF = jnp.bfloat16
F32 = jnp.float32
VMEM = pl.BlockSpec(memory_space=pltpu.VMEM)


def spot(x, y, x2, y2):
    p = y // 2
    return p, x + 1, W * (y - 2 * p + 1), 256 * (x2 - x + 1) + W * (y2 - 2 * p + 1)


def block(dense, x, y, x2, y2):
    p, i, r, c = spot(x, y, x2, y2)
    return dense[p, i, r : r + W, c : c + W]


def triangles():
    row = lax.broadcasted_iota(jnp.int32, (W, W), 0)
    col = lax.broadcasted_iota(jnp.int32, (W, W), 1)
    return [m.astype(F32).astype(BF) for m in (row <= col, row > col, row == col)]


def strip_mask(mask_ref, x):
    slot = lax.broadcasted_iota(jnp.int32, (9, 9 * W), 0)
    lane = lax.broadcasted_iota(jnp.int32, (9, 9 * W), 1)
    spread = (lane // W == slot).astype(BF)
    flags = mask_ref[x].astype(F32).astype(BF)
    return jnp.dot(flags, spread, preferred_element_type=F32)


def window_mask(mask_ref, x):
    slot = lax.broadcasted_iota(jnp.int32, (9, 12 * W), 0)
    lane = lax.broadcasted_iota(jnp.int32, (9, 12 * W), 1)
    flags = mask_ref[x].astype(F32).astype(BF)
    out = []
    for r in range(2):
        dy = (lane % 256) // W - r
        inside = (dy >= 0) & (dy <= 2) & (lane // 256 * 3 + dy == slot)
        out.append(jnp.dot(flags, inside.astype(BF), preferred_element_type=F32))
    return out


def both_rows(wide, x, p):
    return jnp.concatenate(
        [
            jnp.broadcast_to(wide[x, 0, 2 * p : 2 * p + 1, :], (W, 768)),
            jnp.broadcast_to(wide[x, 1, 2 * p + 1 : 2 * p + 2, :], (W, 768)),
        ],
        axis=0,
    )


def put_strips(dst, ref):
    zero = jnp.zeros((W, W), BF)
    for x in range(4):
        for y in range(4):
            strip = ref[x, y]
            p, r = y // 2, y % 2
            for d in range(3):
                piece = strip[:, 192 * d : 192 * d + 192]
                parts = [piece, zero] if r == 0 else [zero, piece]
                dst[p, x + 1, W + W * r : 2 * W + W * r, 256 * d : 256 * d + 256] = (
                    jnp.concatenate(parts, axis=1)
                )


def put_shared(dst):
    zero = jnp.zeros((W, 128), BF)
    for i in range(1, 5):
        for d in range(3):
            c = 256 * d
            dst[1, i, 0:64, c : c + 128] = dst[0, i, 128:192, c + 128 : c + 256]
            dst[1, i, 0:64, c + 128 : c + 256] = zero
            dst[0, i, 192:256, c + 128 : c + 256] = dst[1, i, 64:128, c : c + 128]
            dst[0, i, 192:256, c : c + 128] = zero


def put_y(dst, side, msg, n, masks, add):
    y, halo = (0, -1) if side == 0 else (3, 4)
    same, after, before = line_tiles([line_cell(msg, n, i, 0, masks) for i in range(4)])

    def along(x, x2):
        c, d = x // 2, x2 // 2
        tile = same[c] if c == d else after[0] if c < d else before[0]
        return tile[W * (x % 2) : W * (x % 2) + W, W * (x2 % 2) : W * (x2 % 2) + W]

    for x in range(4):
        for x2 in range(max(0, x - 1), min(3, x + 1) + 1):
            add[W * x : W * x + W, W * x2 : W * x2 + W] = block(dst, x, y, x2, halo)
    inner = add[...].T
    rest = jnp.zeros((W, 128), BF)
    for x in range(4):
        for d in (-1, 0, 1):
            x2 = x + d
            if 0 <= x2 < 4:
                two = along(x, x2), inner[W * x : W * x + W, W * x2 : W * x2 + W]
            elif n == 2:
                continue
            elif x == 0:
                link = msg[6][:, W * n : W * n + W]
                two = link, msg[10][:, W * n : W * n + W]
            else:
                two = msg[3 if n == 0 else 5][:, :W], msg[11][:, W * n : W * n + W]
            parts = [*two, rest] if side == 0 else [rest, two[1], two[0]]
            c = 256 * (d + 1)
            dst[side, x + 1, 192 * side : 192 * side + W, c : c + 256] = jnp.concatenate(parts, axis=1)


def dense_product(left, right, p, x, e, brick=False):
    total = None
    for d in range(max(-1, e - 1), min(1, e + 1) + 1):
        if brick and not 0 <= x + d < 4:
            continue
        term = jnp.dot(
            left[:, 256 * (d + 1) : 256 * (d + 2)],
            right[p, x + 1 + d, :, 256 * (e - d + 1) : 256 * (e - d + 2)],
            preferred_element_type=F32,
        )
        total = term if total is None else total + term
    return total


def line_message(blocks, ends, flags):
    tiles = []
    for get in blocks:
        tiles += [jnp.concatenate([get(i, i), get(i, i + 1)], axis=1) for i in range(4)]
    tiles.append(jnp.concatenate([blocks[0](0, -1), blocks[1](0, -1)], axis=1))
    rows = [jnp.broadcast_to(f, (16, W)).astype(BF) for f in flags]
    tiles.append(jnp.concatenate([blocks[2](0, -1), jnp.concatenate(rows, axis=0)], axis=1))
    for pair in ends:
        tiles.append(jnp.concatenate(pair, axis=1))
    return tiles


def sender(hm, dm, keep):
    def lanes(dx, dy):
        k = 3 * (dx + 1) + dy + 1
        return slice(W * k, W * k + W)

    def flag(x, y, dx, dy):
        return keep[x, y : y + 1, lanes(dx, dy)]

    def get(ref, x, y, dx, dy):
        return ref[x, y, :, lanes(dx, dy)]

    def through(x, y, cells, dx, dy):
        left, right = [], []
        for first, second in ((hm, dm), (dm, hm)):
            for mx, my in cells:
                left.append(get(first, x, y, mx - x, my - y))
                right.append(get(second, mx, my, x + dx - mx, y + dy - my))
        total = jnp.dot(
            jnp.concatenate(left, axis=1), jnp.concatenate(right, axis=0), preferred_element_type=F32
        )
        return (total * flag(x, y, dx, dy)).astype(BF)

    def rows(left, right):
        return lax.dot_general(left, right, (((1,), (1,)), ((), ())), preferred_element_type=F32)

    def own(x, y):
        total = rows(hm[x, y], dm[x, y]) + rows(dm[x, y], hm[x, y])
        return (total * flag(x, y, 0, 0)).astype(BF)

    def link(x, y, dx, dy):
        if dx == 1:
            parts = [(slice(192, 576), slice(0, 384))]
        else:
            parts = [(slice(192 * d + 64, 192 * d + 192), slice(192 * d, 192 * d + 128)) for d in range(3)]
        left, right = [], []
        for first, second in ((hm, dm), (dm, hm)):
            left += [first[x, y, :, one] for one, _ in parts]
            right += [second[x + dx, y + dy, :, other] for _, other in parts]
        total = rows(jnp.concatenate(left, axis=1), jnp.concatenate(right, axis=1))
        return (total * flag(x, y, dx, dy)).astype(BF)

    def pair(one, two, swap=0):
        return jnp.concatenate([two, one] if swap else [one, two], axis=1)

    upper, lower, eye = triangles()
    selfs = {}

    def packed(x, y):
        return get(hm, x, y, 0, 0) * upper + get(dm, x, y, 0, 0) * lower

    def diagonal(value):
        return jnp.sum((value * eye).astype(F32), axis=0, keepdims=True)

    row = lax.broadcasted_iota(jnp.int32, (W, W), 0)
    col = lax.broadcasted_iota(jnp.int32, (W, W), 1)
    def put_line(out, cell, step, marks, first):
        dx, dy = step
        cells = [cell(i) for i in range(4)]
        items = list(marks)
        for i, (x, y) in enumerate(cells):
            out[i] = pair(packed(x, y), get(hm, x, y, dx, dy), (first + i) % 2)
            items.append(diagonal(get(dm, x, y, 0, 0)))
        items += [diagonal(selfs[cells[i]]) for i in (2, 3)]
        even = 1 - first % 2
        for i in range(2):
            one, two = cells[2 * i], cells[2 * i + 1]
            out[4 + i] = pair(get(dm, *one, dx, dy), get(dm, *two, dx, dy), even)
        x, y = cells[0]
        out[6] = pair(get(hm, x, y, -dx, -dy), get(dm, x, y, -dx, -dy))
        mixed = [selfs[cells[i]] * upper + selfs[cells[i + 2]] * lower for i in range(2)]
        out[7] = pair(*mixed, 1 - even)
        out[8] = pair(link(*cells[0], dx, dy), link(*cells[1], dx, dy), even)
        rows = jnp.zeros((16, W), F32)
        for k, item in enumerate(items):
            rows = jnp.where(row[:16] == k, item, rows)
        rows = jnp.concatenate([rows.astype(BF), jnp.zeros((48, W), BF)], axis=0)
        out[9] = pair(link(*cells[2], dx, dy), rows, even)

    return get, flag, through, own, link, pair, packed, diagonal, put_line, selfs, upper, row, col


def send_x_kernel(
    ham, dens, pattern, kept, x_up, x_down, hm, dm, wide, keep, hb, db, pb, kb, live, sems, mask_sems,
):
    masks = [
        pltpu.make_async_copy(pattern, pb, mask_sems.at[0]),
        pltpu.make_async_copy(kept, kb, mask_sems.at[1]),
    ]
    copies = {x: [] for x in (0, 3, 1, 2)}
    for x in copies:
        for n, (ref, buf) in enumerate(((ham, hb), (dens, db))):
            copies[x].append(pltpu.make_async_copy(ref.at[x], buf.at[x], sems.at[n, x]))
    for copy in masks + sum(copies.values(), []):
        copy.start()
    for copy in masks:
        copy.wait()
    for x in range(4):
        live[x] = strip_mask(pb, x)
        keep[x] = strip_mask(kb, x)

    def arrive(x):
        for copy in copies[x]:
            copy.wait()
        for y in range(4):
            mask = live[x, y : y + 1, :].astype(BF)
            hm[x, y] = hb[x, y] * mask
            dm[x, y] = db[x, y] * mask

    _, flag, _, own, _, _, _, _, put_line, selfs, *_ = sender(hm, dm, keep)
    arrive(0)
    arrive(3)
    for x, out, dx in ((0, x_down, -1), (3, x_up, 1)):
        selfs.update({(x, y): own(x, y) for y in range(4)})
        marks = [flag(x, 0, 0, -1), flag(x, 0, dx, -1), flag(x, 3, 0, 1), flag(x, 3, dx, 1)]
        put_line(out, lambda i: (x, i), (0, 1), marks, 1)
    arrive(1)
    arrive(2)
    for x in range(4):
        wide[x, 0], wide[x, 1] = window_mask(kb, x)


def send_y_kernel(hm, dm, keep, ends_up, ends_down, cy_up, cy_down, y_up, y_down):
    get, flag, through, own, _, pair, packed, diagonal, put_line, selfs, upper, row, col = sender(hm, dm, keep)
    selfs.update({(x, y): own(x, y) for x in range(4) for y in (0, 3)})
    ends_up[...] = jnp.zeros_like(ends_up)
    ends_down[...] = jnp.zeros_like(ends_down)
    for y, out, line, dy in ((3, cy_up, y_up, 1), (0, cy_down, y_down, -1)):
        alongs = []
        for n, (x, dx) in enumerate(((0, -1), (3, 1))):
            across = through(x, y, ((x - dx, y),), 0, dy)
            along = through(x, y, ((x, y - dy),), dx, 0)
            alongs.append(along)
            low = diagonal(get(dm, x, y, 0, 0))
            low = jnp.where(row == col + 1, low, jnp.where((row == 63) & (col == 0), low[:, 63:64], 0.0))
            odd = 1 if y == 0 else 0
            out[2 * n] = pair(selfs[x, y] * upper + low.astype(BF), across, odd)
            out[2 * n + 1] = pair(packed(x, y), along.T, odd)
            ends = ends_up if x == 3 else ends_down
            if y == 0:
                ends[0, :, W:] = across.T
            else:
                ends[2, :, 0:W] = across.T
        line[12] = pair(*alongs)

    for y, out, dy in ((3, y_up, 1), (0, y_down, -1)):
        marks = [flag(0, y, -1, 0), flag(0, y, -1, dy), flag(3, y, 1, 0), flag(3, y, 1, dy)]
        put_line(out, lambda i: (i, y), (1, 0), marks, 0)
        for n, (x, dx) in enumerate(((0, -1), (3, 1))):
            out[10 + n] = pair(get(hm, x, y, dx, dy), get(dm, x, y, dx, dy))


def halves(odd):
    row = lax.broadcasted_iota(jnp.int32, (W, 128), 0)
    col = lax.broadcasted_iota(jnp.int32, (W, 128), 1) - W * odd
    mine = (col >= 0) & (col < W)
    masks = (mine & (row <= col), mine & (row > col), mine & (row == col), jnp.logical_not(mine))
    return [m.astype(F32).astype(BF) for m in masks]


def line_cell(msg, n, i, first, masks):
    odd = (first + i) % 2
    upper, lower, eye, other = masks[odd]
    own = msg[i] if n < 2 else msg[7]
    if n == 0:
        link = own * other
    else:
        link = None if n == 2 and i == 3 else msg[4 + 4 * (n - 1) + i // 2] * other
    if n == 1 or n == 2 and i >= 2:
        add = own * lower
        k = 4 + i if n == 1 else 6 + i
        diag = msg[9][k : k + 1, W * (first % 2) : W * (first % 2) + W]
        lay = add + jnp.concatenate([diag, diag], axis=1) * eye
    else:
        lay, add = own * upper, own * (upper - eye)
    if odd or link is None:
        return lay, add, link
    return lay + link, add + link, None


def line_tiles(rows):
    zero = jnp.zeros((W, 128), BF)
    same, after, before = [], [], []
    for c in range(len(rows) // 2):
        one, two = rows[2 * c], rows[2 * c + 1]
        lay = jnp.concatenate([one[0], two[0]], axis=0)
        same.append(lay + jnp.concatenate([one[1], two[1]], axis=0).T)
        if 2 * c + 2 < len(rows):
            after.append(jnp.concatenate([zero, two[2]], axis=0))
            before.append(after[-1].T)
    return same, after, before


def edge(side):
    return (0, 0, 1, 2) if side == 0 else (3, 2, 1, 0)


def part(n):
    return slice(256 * n, 256 * n + 256)


def unpack_rows(total, p, x, e, out):
    cols = slice(192 * (e + 1), 192 * (e + 2))
    out[x, 2 * p, :, cols] = total[0:64, 0:192]
    out[x, 2 * p + 1, :, cols] = total[64:128, 64:256]


def middle_kernel(
    ham, dens, wide, y_low, y_high, out, h_edge, d_edge, h_back, d_back, a_edge, g_edge, done_edge,
    xh, xd, xs, a_rows, rows, add, sems,
):
    ys = (y_low, y_high)
    masks = halves(0), halves(1)
    for n, (ref, dst, keep, turned) in enumerate(
        ((ham, xh, h_edge, h_back), (dens, xd, d_edge, d_back))
    ):
        put_strips(dst, ref)
        put_shared(dst)
        for side in range(2):
            put_y(dst, side, ys[side], n, masks, add.at[2 * side + n])
        for side in range(2):
            x, go, _, back = edge(side)
            for p in range(2):
                tile = dst[p, x + 1, :, part(go)].T
                dst[p, 5 * side, :, part(back)] = tile
                turned[side, p] = tile
                keep[side, p] = dst[p, x + 1]
    for x in range(4):
        for p in range(2):
            mask = both_rows(wide, x, p)
            lh = xh[p, x + 1, 64:192, :]
            ld = xd[p, x + 1, 64:192, :]
            for e in range(-1, 2):
                if 0 <= x + e < 4:
                    cols = part(e + 1)
                    a = dense_product(lh, xd, p, x, e) * mask[:, cols]
                    b = dense_product(ld, xh, p, x, e) * mask[:, cols]
                    a_rows[p, x, :, cols] = a.astype(BF)
                    xs[p, x + 1, 64:192, cols] = (a + b).astype(BF)
    put_shared(xs)
    for side in range(2):
        put_y(xs, side, ys[side], 2, masks, add.at[4 + side])
        for p in range(2):
            x = edge(side)[0]
            a_edge[side, p] = a_rows[p, x, :, part(1)]
    for x in (1, 2, 0, 3):
        for p in range(2):
            mask = both_rows(wide, x, p)
            la = a_rows[p, x]
            ld = xd[p, x + 1, 64:192, :]
            for e in range(-1, 2):
                if not 0 <= x + e < 4:
                    continue
                cols = part(e + 1)
                cubic = dense_product(la, xd, p, x, e, True) + dense_product(ld, xs, p, x, e, True)
                total = 3.0 * xs[p, x + 1, 64:192, cols].astype(F32) - 2.0 * cubic
                if x in (1, 2):
                    unpack_rows((total * mask[:, cols]).astype(BF), p, x - 1, e, rows)
                elif e == 0:
                    g_edge[x // 3, p] = total
                else:
                    done_edge[x // 3, p] = (total * mask[:, cols]).astype(BF)
        if x == 2:
            copy = pltpu.make_async_copy(rows, out.at[1:3], sems.at[0])
            copy.start()
    copy.wait()


def last_kernel(
    wide, y_low, y_high, x_low, x_high, c_low, h_edge, d_edge, h_back, d_back, a_edge, g_edge,
    done_edge, given, out, hh, dh, sh, ss, sb, a_go, rows, sems,
):
    ys, xm, cs = (y_low, y_high), (x_low, x_high), (c_low, x_high.at[10:14])
    both = [(sx, p) for sx in range(2) for p in range(2)]

    masks = halves(0), halves(1)

    def corner_cell(sx, sy, n):
        upper, lower, eye, _ = masks[sy]
        one = cs[sx][2 * sy]
        if n == 2:
            return one * upper, one * (upper - eye), None
        value = cs[sx][2 * sy + 1]
        if n == 0:
            return value * upper, value * (upper - eye), None
        row = lax.broadcasted_iota(jnp.int32, (W, W), 0)
        col = lax.broadcasted_iota(jnp.int32, (W, W), 1)
        spread = one[:, W * sy : W * sy + W].astype(F32)
        low = jnp.sum(jnp.where(row == col + 1, spread, 0.0), axis=0, keepdims=True)
        low += jnp.where(col[0:1] == 63, spread[63:64, 0:1], 0.0)
        below = value * lower
        return below + jnp.concatenate([low, low], axis=1).astype(BF) * eye, below, None

    def tile(ref, sx, p):
        return ref[sx, 128 * p : 128 * p + 256, 128 * p : 128 * p + 256]

    def dot(left, right):
        return jnp.dot(left, right, preferred_element_type=F32)

    def fill(dst, sx, n, crossing):
        rows = [line_cell(xm[sx], n, i, 1, masks) for i in range(4)]
        rows = [corner_cell(sx, 0, n), *rows, corner_cell(sx, 1, n)]
        for place, value in crossing:
            lay, add, rest = rows[place]
            rows[place] = lay + value, add + value, rest
        same, after, before = line_tiles(rows)
        for c in range(3):
            at, to = slice(128 * c, 128 * c + 128), slice(128 * c + 128, 128 * c + 256)
            dst[sx, at, at] = same[c]
            if c < 2:
                dst[sx, at, to] = after[c]
                dst[sx, to, at] = before[c]

    for sx in range(2):
        cross = xm[sx][6]
        fill(hh, sx, 0, [(1, cross * masks[1][3])])
        fill(dh, sx, 1, [(1, jnp.concatenate([cross[:, W:], jnp.zeros((W, W), BF)], axis=1))])
    for sx, p in both:
        x, go, _, back = edge(sx)
        mask = both_rows(wide, x, p)[:, part(go)]

        def to_halo(left, right, halo):
            left = left[sx, p, 64:192, :]
            return dot(left[:, part(go)], tile(halo, sx, p)) + dot(
                left[:, part(1)], right[sx, p, :, part(go)]
            )

        a = to_halo(h_edge, d_edge, dh) * mask
        b = to_halo(d_edge, h_edge, hh) * mask
        a_go[sx, p] = a.astype(BF)
        ss[sx, p, 64:192, :] = (a + b).astype(BF)
    z2 = jnp.zeros((W, 128), BF)
    ab = {}
    for sx, sy in both:
        x, go, _, back = edge(sx)
        two = slice(128 * sy, 128 * sy + 128)
        hp, ep = (0, 1) if sy == 0 else (1, 0)

        def four(row, halo, back_tile):
            def cols(n):
                return slice(256 * n + 128 * sy, 256 * n + 128 * sy + 128)

            top = [tile(halo, sx, sy)[two, two], back_tile[sx, sy, two, two]]
            low = [row[sx, sy, two, cols(go)], row[sx, sy, two, cols(1)]]
            return jnp.concatenate(
                [jnp.concatenate(top, axis=1), jnp.concatenate(low, axis=1)], axis=0
            )

        qh, qd = four(h_edge, hh, h_back), four(d_edge, dh, d_back)
        q = dot(jnp.concatenate([qh, qd], axis=1), jnp.concatenate([qd, qh], axis=0))

        def blk(i, j):
            return q[W * i : W * i + W, W * j : W * j + W]

        a, b, c = hp, ep, 2 + hp
        xt, yt = xm[sx], ys[sy]
        keep_ba = xt[9][2 * sy : 2 * sy + 1, W:].astype(F32)
        keep_bc = xt[9][2 * sy + 1 : 2 * sy + 2, W:].astype(F32)
        keep_ca = yt[9][2 * sx : 2 * sx + 1, :W].astype(F32)
        rest = slice(W * (1 - sy), W * (1 - sy) + W)
        given_ab, given_ca = cs[sx][2 * sy][:, rest], cs[sx][2 * sy + 1][:, rest]
        ab[sx, sy] = (given_ab.astype(F32) + keep_ba * blk(a, b)).astype(BF)
        ca = yt[12][:, W * sx : W * sx + W].astype(F32) + given_ca.astype(F32) + keep_ca * blk(c, a)
        ca, cb = ca.astype(BF), (keep_bc * blk(c, b)).astype(BF)
        here = slice(192 * sy, 192 * sy + W)
        ss[sx, sy, here, :] = jnp.concatenate([ca, cb, z2] if sy == 0 else [z2, cb, ca], axis=1)
    for sx in range(2):
        ss[sx, 1, 0:64, :] = jnp.concatenate([ss[sx, 0, 128:192, 128:256], z2], axis=1)
        ss[sx, 0, 192:256, :] = jnp.concatenate([z2, ss[sx, 1, 64:128, 0:128]], axis=1)

        none = jnp.zeros((W, W), BF)
        crossing = [
            (0, jnp.concatenate([none, ab[sx, 0]], axis=1)),
            (5, jnp.concatenate([ab[sx, 1], none], axis=1)),
        ]
        fill(sh, sx, 2, crossing)
        for p in range(2):
            sb[sx, p] = ss[sx, p].T
    copies = []
    for sx, p in both:
        x, go, _, back = edge(sx)
        mask = both_rows(wide, x, p)
        ld = d_edge[sx, p, 64:192, :]
        outer = dot(a_go[sx, p], tile(dh, sx, p)) + dot(ld[:, part(go)], tile(sh, sx, p))
        outer += dot(a_edge[sx, p], d_edge[sx, p, :, part(go)]) + dot(ld[:, part(1)], ss[sx, p])
        outer = 3.0 * ss[sx, p, 64:192, :].astype(F32) - 2.0 * outer
        same = dot(a_go[sx, p], d_back[sx, p]) + dot(ld[:, part(go)], sb[sx, p])
        same = g_edge[sx, p] - 2.0 * same
        unpack_rows((outer * mask[:, part(go)]).astype(BF), p, sx, go - 1, rows)
        unpack_rows((same * mask[:, part(1)]).astype(BF), p, sx, 0, rows)
        unpack_rows(done_edge[sx, p], p, sx, back - 1, rows)
        if p == 1:
            copies.append(pltpu.make_async_copy(rows.at[sx], out.at[x], sems.at[sx]))
            copies[-1].start()
    for copy in copies:
        copy.wait()


ANY = pl.BlockSpec(memory_space=pl.ANY)


def call(kernel, outs, scratch, inputs, limit, spaces=None, aliases=None):
    def shape(s):
        return s if isinstance(s, jax.ShapeDtypeStruct) else jax.ShapeDtypeStruct(s, BF)

    return pl.pallas_call(
        kernel,
        out_shape=[shape(s) for s in outs],
        in_specs=inputs,
        out_specs=spaces or [VMEM] * len(outs),
        scratch_shapes=[pltpu.VMEM(s, BF) if isinstance(s, tuple) else s for s in scratch],
        input_output_aliases=aliases or {},
        compiler_params=pltpu.CompilerParams(vmem_limit_bytes=limit * 1024 * 1024),
    )


def shift(value, axis, step):
    count = lax.axis_size(axis)
    return lax.ppermute(value, axis, [(i, (i + step) % count) for i in range(count)])


def per_device(ham, dens, pattern, kept):
    dense = (2, 6, 256, 768)
    corner, y_line, x_line = (4, W, 128), (13, W, 128), (10, W, 128)
    mask = pltpu.VMEM(pattern.shape, pattern.dtype)
    flags = pltpu.VMEM((4, 4, 9 * W), F32)
    inputs = [pltpu.with_memory_space_constraint(v, pltpu.HBM) for v in (ham, dens, pattern, kept)]
    keep = jax.ShapeDtypeStruct((4, 4, 9 * W), F32)
    x_up, x_down, ham, dens, wide, keep = call(
        send_x_kernel,
        [x_line, x_line, ham.shape, dens.shape, jax.ShapeDtypeStruct((4, 2, 4, 12 * W), F32), keep],
        [ham.shape, dens.shape, mask, mask, flags]
        + [pltpu.SemaphoreType.DMA((2, 4)), pltpu.SemaphoreType.DMA((2,))],
        [ANY] * 4,
        16,
    )(*inputs)
    ends_up, ends_down, cy_up, cy_down, y_up, y_down = call(
        send_y_kernel, [corner] * 4 + [y_line] * 2, [], [VMEM] * 3, 16
    )(ham, dens, keep)
    cy_low = shift(cy_up, "gy", 1)
    cy_high = shift(cy_down, "gy", -1)
    y_low = shift(y_up, "gy", 1)
    y_high = shift(y_down, "gy", -1)
    x_low = shift(x_up, "gx", 1)

    def forward(n, ends):
        at = slice(2 * n, 2 * n + 2)
        return jnp.concatenate([cy_low[at], cy_high[at]]) + ends

    x_high = shift(jnp.concatenate([x_down, forward(0, ends_down)]), "gx", -1)
    c_low = shift(forward(1, ends_up), "gx", 1)
    edges = [(2, 2, 256, 768)] * 2 + [(2, 2, 256, 256)] * 2 + [(2, 2, 128, 256)]
    edges += [jax.ShapeDtypeStruct((2, 2, 128, 256), F32), (2, 2, 128, 256)]
    out, *edges = call(
        middle_kernel,
        [ham.shape] + edges,
        [dense] * 3 + [(2, 4, 128, 768), (2, 4, W, 9 * W)]
        + [(6, 256, 256)]
        + [pltpu.SemaphoreType.DMA((1,))],
        [VMEM] * 5,
        32,
        [ANY] + [VMEM] * 7,
    )(ham, dens, wide, y_low, y_high)
    six, tile, rows = (2, 384, 384), (2, 2, 256, 256), (2, 4, W, 9 * W)
    return call(
        last_kernel,
        [ham.shape],
        [six] * 3
        + [tile] * 2
        + [(2, 2, 128, 256), rows, pltpu.SemaphoreType.DMA((2,))],
        [VMEM] * 13 + [ANY],
        32,
        [ANY],
        {13: 0},
    )(wide, y_low, y_high, x_low, x_high, c_low, *edges, out)[0]


def solution(mesh):
    return jax.shard_map(
        per_device,
        mesh=mesh,
        in_specs=(
            P("gx", "gy", None, None),
            P("gx", "gy", None, None),
            P("gx", "gy", None),
            P("gx", "gy", None),
        ),
        out_specs=P("gx", "gy", None, None),
        check_vma=False,
    )
```

```python
import jax
import jax.numpy as jnp
from jax import lax
from jax.experimental import pallas as pl
from jax.experimental.pallas import tpu as pltpu
from jax.sharding import PartitionSpec as P

W = 64
BF = jnp.bfloat16
F32 = jnp.float32
VMEM = pl.BlockSpec(memory_space=pltpu.VMEM)


def spot(x, y, x2, y2):
    p = y // 2
    return p, x + 1, W * (y - 2 * p + 1), 256 * (x2 - x + 1) + W * (y2 - 2 * p + 1)


def block(dense, x, y, x2, y2):
    p, i, r, c = spot(x, y, x2, y2)
    return dense[p, i, r : r + W, c : c + W]


def triangles():
    row = lax.broadcasted_iota(jnp.int32, (W, W), 0)
    col = lax.broadcasted_iota(jnp.int32, (W, W), 1)
    return [m.astype(F32).astype(BF) for m in (row <= col, row > col, row == col)]


def strip_mask(mask_ref, x):
    slot = lax.broadcasted_iota(jnp.int32, (9, 9 * W), 0)
    lane = lax.broadcasted_iota(jnp.int32, (9, 9 * W), 1)
    spread = (lane // W == slot).astype(BF)
    flags = mask_ref[x].astype(F32).astype(BF)
    return jnp.dot(flags, spread, preferred_element_type=F32)


def window_mask(mask_ref, x):
    slot = lax.broadcasted_iota(jnp.int32, (9, 12 * W), 0)
    lane = lax.broadcasted_iota(jnp.int32, (9, 12 * W), 1)
    flags = mask_ref[x].astype(F32).astype(BF)
    out = []
    for r in range(2):
        dy = (lane % 256) // W - r
        inside = (dy >= 0) & (dy <= 2) & (lane // 256 * 3 + dy == slot)
        out.append(jnp.dot(flags, inside.astype(BF), preferred_element_type=F32))
    return out


def both_rows(wide, x, p):
    return jnp.concatenate(
        [
            jnp.broadcast_to(wide[x, 0, 2 * p : 2 * p + 1, :], (W, 768)),
            jnp.broadcast_to(wide[x, 1, 2 * p + 1 : 2 * p + 2, :], (W, 768)),
        ],
        axis=0,
    )


def put_strips(dst, ref):
    zero = jnp.zeros((W, W), BF)
    for x in range(4):
        for y in range(4):
            strip = ref[x, y]
            p, r = y // 2, y % 2
            for d in range(3):
                piece = strip[:, 192 * d : 192 * d + 192]
                parts = [piece, zero] if r == 0 else [zero, piece]
                dst[p, x + 1, W + W * r : 2 * W + W * r, 256 * d : 256 * d + 256] = (
                    jnp.concatenate(parts, axis=1)
                )


def put_shared(dst):
    zero = jnp.zeros((W, 128), BF)
    for i in range(1, 5):
        for d in range(3):
            c = 256 * d
            dst[1, i, 0:64, c : c + 128] = dst[0, i, 128:192, c + 128 : c + 256]
            dst[1, i, 0:64, c + 128 : c + 256] = zero
            dst[0, i, 192:256, c + 128 : c + 256] = dst[1, i, 64:128, c : c + 128]
            dst[0, i, 192:256, c : c + 128] = zero


def put_y(dst, side, msg, n, masks, add):
    y, halo = (0, -1) if side == 0 else (3, 4)
    same, after, before = line_tiles([line_cell(msg, n, i, 0, masks) for i in range(4)])

    def along(x, x2):
        c, d = x // 2, x2 // 2
        tile = same[c] if c == d else after[0] if c < d else before[0]
        return tile[W * (x % 2) : W * (x % 2) + W, W * (x2 % 2) : W * (x2 % 2) + W]

    for x in range(4):
        for x2 in range(max(0, x - 1), min(3, x + 1) + 1):
            add[W * x : W * x + W, W * x2 : W * x2 + W] = block(dst, x, y, x2, halo)
    inner = add[...].T
    rest = jnp.zeros((W, 128), BF)
    for x in range(4):
        for d in (-1, 0, 1):
            x2 = x + d
            if 0 <= x2 < 4:
                two = along(x, x2), inner[W * x : W * x + W, W * x2 : W * x2 + W]
            elif n == 2:
                continue
            elif x == 0:
                link = msg[6][:, W * n : W * n + W]
                two = link, msg[10][:, W * n : W * n + W]
            else:
                two = msg[3 if n == 0 else 5][:, :W], msg[11][:, W * n : W * n + W]
            parts = [*two, rest] if side == 0 else [rest, two[1], two[0]]
            c = 256 * (d + 1)
            dst[side, x + 1, 192 * side : 192 * side + W, c : c + 256] = jnp.concatenate(parts, axis=1)


def dense_product(left, right, p, x, e, brick=False):
    total = None
    for d in range(max(-1, e - 1), min(1, e + 1) + 1):
        if brick and not 0 <= x + d < 4:
            continue
        term = jnp.dot(
            left[:, 256 * (d + 1) : 256 * (d + 2)],
            right[p, x + 1 + d, :, 256 * (e - d + 1) : 256 * (e - d + 2)],
            preferred_element_type=F32,
        )
        total = term if total is None else total + term
    return total


def line_message(blocks, ends, flags):
    tiles = []
    for get in blocks:
        tiles += [jnp.concatenate([get(i, i), get(i, i + 1)], axis=1) for i in range(4)]
    tiles.append(jnp.concatenate([blocks[0](0, -1), blocks[1](0, -1)], axis=1))
    rows = [jnp.broadcast_to(f, (16, W)).astype(BF) for f in flags]
    tiles.append(jnp.concatenate([blocks[2](0, -1), jnp.concatenate(rows, axis=0)], axis=1))
    for pair in ends:
        tiles.append(jnp.concatenate(pair, axis=1))
    return tiles


def sender(hm, dm, keep):
    def lanes(dx, dy):
        k = 3 * (dx + 1) + dy + 1
        return slice(W * k, W * k + W)

    def flag(x, y, dx, dy):
        return keep[x, y : y + 1, lanes(dx, dy)]

    def get(ref, x, y, dx, dy):
        return ref[x, y, :, lanes(dx, dy)]

    def through(x, y, cells, dx, dy):
        left, right = [], []
        for first, second in ((hm, dm), (dm, hm)):
            for mx, my in cells:
                left.append(get(first, x, y, mx - x, my - y))
                right.append(get(second, mx, my, x + dx - mx, y + dy - my))
        total = jnp.dot(
            jnp.concatenate(left, axis=1), jnp.concatenate(right, axis=0), preferred_element_type=F32
        )
        return (total * flag(x, y, dx, dy)).astype(BF)

    def rows(left, right):
        return lax.dot_general(left, right, (((1,), (1,)), ((), ())), preferred_element_type=F32)

    def own(x, y):
        total = rows(hm[x, y], dm[x, y]) + rows(dm[x, y], hm[x, y])
        return (total * flag(x, y, 0, 0)).astype(BF)

    def link(x, y, dx, dy):
        if dx == 1:
            parts = [(slice(192, 576), slice(0, 384))]
        else:
            parts = [(slice(192 * d + 64, 192 * d + 192), slice(192 * d, 192 * d + 128)) for d in range(3)]
        left, right = [], []
        for first, second in ((hm, dm), (dm, hm)):
            left += [first[x, y, :, one] for one, _ in parts]
            right += [second[x + dx, y + dy, :, other] for _, other in parts]
        total = rows(jnp.concatenate(left, axis=1), jnp.concatenate(right, axis=1))
        return (total * flag(x, y, dx, dy)).astype(BF)

    def pair(one, two, swap=0):
        return jnp.concatenate([two, one] if swap else [one, two], axis=1)

    upper, lower, eye = triangles()
    selfs = {}

    def packed(x, y):
        return get(hm, x, y, 0, 0) * upper + get(dm, x, y, 0, 0) * lower

    def diagonal(value):
        return jnp.sum((value * eye).astype(F32), axis=0, keepdims=True)

    row = lax.broadcasted_iota(jnp.int32, (W, W), 0)
    col = lax.broadcasted_iota(jnp.int32, (W, W), 1)
    def put_line(out, cell, step, marks, first):
        dx, dy = step
        cells = [cell(i) for i in range(4)]
        items = list(marks)
        for i, (x, y) in enumerate(cells):
            out[i] = pair(packed(x, y), get(hm, x, y, dx, dy), (first + i) % 2)
            items.append(diagonal(get(dm, x, y, 0, 0)))
        items += [diagonal(selfs[cells[i]]) for i in (2, 3)]
        even = 1 - first % 2
        for i in range(2):
            one, two = cells[2 * i], cells[2 * i + 1]
            out[4 + i] = pair(get(dm, *one, dx, dy), get(dm, *two, dx, dy), even)
        x, y = cells[0]
        out[6] = pair(get(hm, x, y, -dx, -dy), get(dm, x, y, -dx, -dy))
        mixed = [selfs[cells[i]] * upper + selfs[cells[i + 2]] * lower for i in range(2)]
        out[7] = pair(*mixed, 1 - even)
        out[8] = pair(link(*cells[0], dx, dy), link(*cells[1], dx, dy), even)
        rows = jnp.zeros((16, W), F32)
        for k, item in enumerate(items):
            rows = jnp.where(row[:16] == k, item, rows)
        rows = jnp.concatenate([rows.astype(BF), jnp.zeros((48, W), BF)], axis=0)
        out[9] = pair(link(*cells[2], dx, dy), rows, even)

    return get, flag, through, own, link, pair, packed, diagonal, put_line, selfs, upper, row, col


def send_x_kernel(
    ham, dens, pattern, kept, x_up, x_down, hm, dm, wide, keep, hb, db, pb, kb, live, sems, mask_sems,
):
    masks = [
        pltpu.make_async_copy(pattern, pb, mask_sems.at[0]),
        pltpu.make_async_copy(kept, kb, mask_sems.at[1]),
    ]
    copies = {x: [] for x in (0, 3, 1, 2)}
    for x in copies:
        for n, (ref, buf) in enumerate(((ham, hb), (dens, db))):
            copies[x].append(pltpu.make_async_copy(ref.at[x], buf.at[x], sems.at[n, x]))
    for copy in masks + sum(copies.values(), []):
        copy.start()
    for copy in masks:
        copy.wait()
    for x in range(4):
        live[x] = strip_mask(pb, x)
        keep[x] = strip_mask(kb, x)

    def arrive(x):
        for copy in copies[x]:
            copy.wait()
        for y in range(4):
            mask = live[x, y : y + 1, :].astype(BF)
            hm[x, y] = hb[x, y] * mask
            dm[x, y] = db[x, y] * mask

    _, flag, _, own, _, _, _, _, put_line, selfs, *_ = sender(hm, dm, keep)
    arrive(0)
    arrive(3)
    for x, out, dx in ((0, x_down, -1), (3, x_up, 1)):
        selfs.update({(x, y): own(x, y) for y in range(4)})
        marks = [flag(x, 0, 0, -1), flag(x, 0, dx, -1), flag(x, 3, 0, 1), flag(x, 3, dx, 1)]
        put_line(out, lambda i: (x, i), (0, 1), marks, 1)
    arrive(1)
    arrive(2)
    for x in range(4):
        wide[x, 0], wide[x, 1] = window_mask(kb, x)


def send_y_kernel(hm, dm, keep, ends_up, ends_down, cy_up, cy_down, y_up, y_down):
    get, flag, through, own, _, pair, packed, diagonal, put_line, selfs, upper, row, col = sender(hm, dm, keep)
    selfs.update({(x, y): own(x, y) for x in range(4) for y in (0, 3)})
    ends_up[...] = jnp.zeros_like(ends_up)
    ends_down[...] = jnp.zeros_like(ends_down)
    for y, out, line, dy in ((3, cy_up, y_up, 1), (0, cy_down, y_down, -1)):
        alongs = []
        for n, (x, dx) in enumerate(((0, -1), (3, 1))):
            across = through(x, y, ((x - dx, y),), 0, dy)
            along = through(x, y, ((x, y - dy),), dx, 0)
            alongs.append(along)
            low = diagonal(get(dm, x, y, 0, 0))
            low = jnp.where(row == col + 1, low, jnp.where((row == 63) & (col == 0), low[:, 63:64], 0.0))
            odd = 1 if y == 0 else 0
            out[2 * n] = pair(selfs[x, y] * upper + low.astype(BF), across, odd)
            out[2 * n + 1] = pair(packed(x, y), along.T, odd)
            ends = ends_up if x == 3 else ends_down
            if y == 0:
                ends[0, :, W:] = across.T
            else:
                ends[2, :, 0:W] = across.T
        line[12] = pair(*alongs)

    for y, out, dy in ((3, y_up, 1), (0, y_down, -1)):
        marks = [flag(0, y, -1, 0), flag(0, y, -1, dy), flag(3, y, 1, 0), flag(3, y, 1, dy)]
        put_line(out, lambda i: (i, y), (1, 0), marks, 0)
        for n, (x, dx) in enumerate(((0, -1), (3, 1))):
            out[10 + n] = pair(get(hm, x, y, dx, dy), get(dm, x, y, dx, dy))


def halves(odd):
    row = lax.broadcasted_iota(jnp.int32, (W, 128), 0)
    col = lax.broadcasted_iota(jnp.int32, (W, 128), 1) - W * odd
    mine = (col >= 0) & (col < W)
    masks = (mine & (row <= col), mine & (row > col), mine & (row == col), jnp.logical_not(mine))
    return [m.astype(F32).astype(BF) for m in masks]


def line_cell(msg, n, i, first, masks):
    odd = (first + i) % 2
    upper, lower, eye, other = masks[odd]
    own = msg[i] if n < 2 else msg[7]
    if n == 0:
        link = own * other
    else:
        link = None if n == 2 and i == 3 else msg[4 + 4 * (n - 1) + i // 2] * other
    if n == 1 or n == 2 and i >= 2:
        add = own * lower
        k = 4 + i if n == 1 else 6 + i
        diag = msg[9][k : k + 1, W * (first % 2) : W * (first % 2) + W]
        lay = add + jnp.concatenate([diag, diag], axis=1) * eye
    else:
        lay, add = own * upper, own * (upper - eye)
    if odd or link is None:
        return lay, add, link
    return lay + link, add + link, None


def line_tiles(rows):
    zero = jnp.zeros((W, 128), BF)
    same, after, before = [], [], []
    for c in range(len(rows) // 2):
        one, two = rows[2 * c], rows[2 * c + 1]
        lay = jnp.concatenate([one[0], two[0]], axis=0)
        same.append(lay + jnp.concatenate([one[1], two[1]], axis=0).T)
        if 2 * c + 2 < len(rows):
            after.append(jnp.concatenate([zero, two[2]], axis=0))
            before.append(after[-1].T)
    return same, after, before


def edge(side):
    return (0, 0, 1, 2) if side == 0 else (3, 2, 1, 0)


def part(n):
    return slice(256 * n, 256 * n + 256)


def unpack_rows(total, p, x, e, out):
    cols = slice(192 * (e + 1), 192 * (e + 2))
    out[x, 2 * p, :, cols] = total[0:64, 0:192]
    out[x, 2 * p + 1, :, cols] = total[64:128, 64:256]


def middle_kernel(
    ham, dens, wide, y_low, y_high, out, h_edge, d_edge, h_back, d_back, a_edge, g_edge, done_edge,
    xh, xd, xs, a_rows, rows, add, sems,
):
    ys = (y_low, y_high)
    masks = halves(0), halves(1)
    for n, (ref, dst, keep, turned) in enumerate(
        ((ham, xh, h_edge, h_back), (dens, xd, d_edge, d_back))
    ):
        put_strips(dst, ref)
        put_shared(dst)
        for side in range(2):
            put_y(dst, side, ys[side], n, masks, add.at[2 * side + n])
        for side in range(2):
            x, go, _, back = edge(side)
            for p in range(2):
                tile = dst[p, x + 1, :, part(go)].T
                dst[p, 5 * side, :, part(back)] = tile
                turned[side, p] = tile
                keep[side, p] = dst[p, x + 1]
    for x in range(4):
        for p in range(2):
            mask = both_rows(wide, x, p)
            lh = xh[p, x + 1, 64:192, :]
            ld = xd[p, x + 1, 64:192, :]
            for e in range(-1, 2):
                if 0 <= x + e < 4:
                    cols = part(e + 1)
                    a = dense_product(lh, xd, p, x, e) * mask[:, cols]
                    b = dense_product(ld, xh, p, x, e) * mask[:, cols]
                    a_rows[p, x, :, cols] = a.astype(BF)
                    xs[p, x + 1, 64:192, cols] = (a + b).astype(BF)
    put_shared(xs)
    for side in range(2):
        put_y(xs, side, ys[side], 2, masks, add.at[4 + side])
        for p in range(2):
            x = edge(side)[0]
            a_edge[side, p] = a_rows[p, x, :, part(1)]
    for x in (1, 2, 0, 3):
        for p in range(2):
            mask = both_rows(wide, x, p)
            la = a_rows[p, x]
            ld = xd[p, x + 1, 64:192, :]
            for e in range(-1, 2):
                if not 0 <= x + e < 4:
                    continue
                cols = part(e + 1)
                cubic = dense_product(la, xd, p, x, e, True) + dense_product(ld, xs, p, x, e, True)
                total = 3.0 * xs[p, x + 1, 64:192, cols].astype(F32) - 2.0 * cubic
                if x in (1, 2):
                    unpack_rows((total * mask[:, cols]).astype(BF), p, x - 1, e, rows)
                elif e == 0:
                    g_edge[x // 3, p] = total
                else:
                    done_edge[x // 3, p] = (total * mask[:, cols]).astype(BF)
        if x == 2:
            copy = pltpu.make_async_copy(rows, out.at[1:3], sems.at[0])
            copy.start()
    copy.wait()


def last_kernel(
    wide, y_low, y_high, x_low, x_high, c_low, h_edge, d_edge, h_back, d_back, a_edge, g_edge,
    done_edge, given, out, hh, dh, sh, ss, sb, a_go, rows, sems,
):
    ys, xm, cs = (y_low, y_high), (x_low, x_high), (c_low, x_high.at[10:14])
    both = [(sx, p) for sx in range(2) for p in range(2)]

    masks = halves(0), halves(1)

    def corner_cell(sx, sy, n):
        upper, lower, eye, _ = masks[sy]
        one = cs[sx][2 * sy]
        if n == 2:
            return one * upper, one * (upper - eye), None
        value = cs[sx][2 * sy + 1]
        if n == 0:
            return value * upper, value * (upper - eye), None
        row = lax.broadcasted_iota(jnp.int32, (W, W), 0)
        col = lax.broadcasted_iota(jnp.int32, (W, W), 1)
        spread = one[:, W * sy : W * sy + W].astype(F32)
        low = jnp.sum(jnp.where(row == col + 1, spread, 0.0), axis=0, keepdims=True)
        low += jnp.where(col[0:1] == 63, spread[63:64, 0:1], 0.0)
        below = value * lower
        return below + jnp.concatenate([low, low], axis=1).astype(BF) * eye, below, None

    def tile(ref, sx, p):
        return ref[sx, 128 * p : 128 * p + 256, 128 * p : 128 * p + 256]

    def dot(left, right):
        return jnp.dot(left, right, preferred_element_type=F32)

    def fill(dst, sx, n, crossing):
        rows = [line_cell(xm[sx], n, i, 1, masks) for i in range(4)]
        rows = [corner_cell(sx, 0, n), *rows, corner_cell(sx, 1, n)]
        for place, value in crossing:
            lay, add, rest = rows[place]
            rows[place] = lay + value, add + value, rest
        same, after, before = line_tiles(rows)
        for c in range(3):
            at, to = slice(128 * c, 128 * c + 128), slice(128 * c + 128, 128 * c + 256)
            dst[sx, at, at] = same[c]
            if c < 2:
                dst[sx, at, to] = after[c]
                dst[sx, to, at] = before[c]

    for sx in range(2):
        cross = xm[sx][6]
        fill(hh, sx, 0, [(1, cross * masks[1][3])])
        fill(dh, sx, 1, [(1, jnp.concatenate([cross[:, W:], jnp.zeros((W, W), BF)], axis=1))])
    for sx, p in both:
        x, go, _, back = edge(sx)
        mask = both_rows(wide, x, p)[:, part(go)]

        def to_halo(left, right, halo):
            left = left[sx, p, 64:192, :]
            return dot(left[:, part(go)], tile(halo, sx, p)) + dot(
                left[:, part(1)], right[sx, p, :, part(go)]
            )

        a = to_halo(h_edge, d_edge, dh) * mask
        b = to_halo(d_edge, h_edge, hh) * mask
        a_go[sx, p] = a.astype(BF)
        ss[sx, p, 64:192, :] = (a + b).astype(BF)
    z2 = jnp.zeros((W, 128), BF)
    ab = {}
    for sx, sy in both:
        x, go, _, back = edge(sx)
        two = slice(128 * sy, 128 * sy + 128)
        hp, ep = (0, 1) if sy == 0 else (1, 0)

        def four(row, halo, back_tile):
            def cols(n):
                return slice(256 * n + 128 * sy, 256 * n + 128 * sy + 128)

            top = [tile(halo, sx, sy)[two, two], back_tile[sx, sy, two, two]]
            low = [row[sx, sy, two, cols(go)], row[sx, sy, two, cols(1)]]
            return jnp.concatenate(
                [jnp.concatenate(top, axis=1), jnp.concatenate(low, axis=1)], axis=0
            )

        qh, qd = four(h_edge, hh, h_back), four(d_edge, dh, d_back)
        q = dot(jnp.concatenate([qh, qd], axis=1), jnp.concatenate([qd, qh], axis=0))

        def blk(i, j):
            return q[W * i : W * i + W, W * j : W * j + W]

        a, b, c = hp, ep, 2 + hp
        xt, yt = xm[sx], ys[sy]
        keep_ba = xt[9][2 * sy : 2 * sy + 1, W:].astype(F32)
        keep_bc = xt[9][2 * sy + 1 : 2 * sy + 2, W:].astype(F32)
        keep_ca = yt[9][2 * sx : 2 * sx + 1, :W].astype(F32)
        rest = slice(W * (1 - sy), W * (1 - sy) + W)
        given_ab, given_ca = cs[sx][2 * sy][:, rest], cs[sx][2 * sy + 1][:, rest]
        ab[sx, sy] = (given_ab.astype(F32) + keep_ba * blk(a, b)).astype(BF)
        ca = yt[12][:, W * sx : W * sx + W].astype(F32) + given_ca.astype(F32) + keep_ca * blk(c, a)
        ca, cb = ca.astype(BF), (keep_bc * blk(c, b)).astype(BF)
        here = slice(192 * sy, 192 * sy + W)
        ss[sx, sy, here, :] = jnp.concatenate([ca, cb, z2] if sy == 0 else [z2, cb, ca], axis=1)
    for sx in range(2):
        ss[sx, 1, 0:64, :] = jnp.concatenate([ss[sx, 0, 128:192, 128:256], z2], axis=1)
        ss[sx, 0, 192:256, :] = jnp.concatenate([z2, ss[sx, 1, 64:128, 0:128]], axis=1)

        none = jnp.zeros((W, W), BF)
        crossing = [
            (0, jnp.concatenate([none, ab[sx, 0]], axis=1)),
            (5, jnp.concatenate([ab[sx, 1], none], axis=1)),
        ]
        fill(sh, sx, 2, crossing)
        for p in range(2):
            sb[sx, p] = ss[sx, p].T
    copies = []
    for sx, p in both:
        x, go, _, back = edge(sx)
        mask = both_rows(wide, x, p)
        ld = d_edge[sx, p, 64:192, :]
        outer = dot(a_go[sx, p], tile(dh, sx, p)) + dot(ld[:, part(go)], tile(sh, sx, p))
        outer += dot(a_edge[sx, p], d_edge[sx, p, :, part(go)]) + dot(ld[:, part(1)], ss[sx, p])
        outer = 3.0 * ss[sx, p, 64:192, :].astype(F32) - 2.0 * outer
        same = dot(a_go[sx, p], d_back[sx, p]) + dot(ld[:, part(go)], sb[sx, p])
        same = g_edge[sx, p] - 2.0 * same
        unpack_rows((outer * mask[:, part(go)]).astype(BF), p, sx, go - 1, rows)
        unpack_rows((same * mask[:, part(1)]).astype(BF), p, sx, 0, rows)
        unpack_rows(done_edge[sx, p], p, sx, back - 1, rows)
        two = slice(2 * p, 2 * p + 2)
        copies.append(pltpu.make_async_copy(rows.at[sx, two], out.at[x, two], sems.at[sx, p]))
        copies[-1].start()
    for copy in copies:
        copy.wait()


ANY = pl.BlockSpec(memory_space=pl.ANY)


def call(kernel, outs, scratch, inputs, limit, spaces=None, aliases=None):
    def shape(s):
        return s if isinstance(s, jax.ShapeDtypeStruct) else jax.ShapeDtypeStruct(s, BF)

    return pl.pallas_call(
        kernel,
        out_shape=[shape(s) for s in outs],
        in_specs=inputs,
        out_specs=spaces or [VMEM] * len(outs),
        scratch_shapes=[pltpu.VMEM(s, BF) if isinstance(s, tuple) else s for s in scratch],
        input_output_aliases=aliases or {},
        compiler_params=pltpu.CompilerParams(vmem_limit_bytes=limit * 1024 * 1024),
    )


def shift(value, axis, step):
    count = lax.axis_size(axis)
    return lax.ppermute(value, axis, [(i, (i + step) % count) for i in range(count)])


def per_device(ham, dens, pattern, kept):
    dense = (2, 6, 256, 768)
    corner, y_line, x_line = (4, W, 128), (13, W, 128), (10, W, 128)
    mask = pltpu.VMEM(pattern.shape, pattern.dtype)
    flags = pltpu.VMEM((4, 4, 9 * W), F32)
    inputs = [pltpu.with_memory_space_constraint(v, pltpu.HBM) for v in (ham, dens, pattern, kept)]
    keep = jax.ShapeDtypeStruct((4, 4, 9 * W), F32)
    x_up, x_down, ham, dens, wide, keep = call(
        send_x_kernel,
        [x_line, x_line, ham.shape, dens.shape, jax.ShapeDtypeStruct((4, 2, 4, 12 * W), F32), keep],
        [ham.shape, dens.shape, mask, mask, flags]
        + [pltpu.SemaphoreType.DMA((2, 4)), pltpu.SemaphoreType.DMA((2,))],
        [ANY] * 4,
        16,
    )(*inputs)
    ends_up, ends_down, cy_up, cy_down, y_up, y_down = call(
        send_y_kernel, [corner] * 4 + [y_line] * 2, [], [VMEM] * 3, 16
    )(ham, dens, keep)
    cy_low = shift(cy_up, "gy", 1)
    cy_high = shift(cy_down, "gy", -1)
    y_low = shift(y_up, "gy", 1)
    y_high = shift(y_down, "gy", -1)
    x_low = shift(x_up, "gx", 1)

    def forward(n, ends):
        at = slice(2 * n, 2 * n + 2)
        return jnp.concatenate([cy_low[at], cy_high[at]]) + ends

    x_high = shift(jnp.concatenate([x_down, forward(0, ends_down)]), "gx", -1)
    c_low = shift(forward(1, ends_up), "gx", 1)
    edges = [(2, 2, 256, 768)] * 2 + [(2, 2, 256, 256)] * 2 + [(2, 2, 128, 256)]
    edges += [jax.ShapeDtypeStruct((2, 2, 128, 256), F32), (2, 2, 128, 256)]
    out, *edges = call(
        middle_kernel,
        [ham.shape] + edges,
        [dense] * 3 + [(2, 4, 128, 768), (2, 4, W, 9 * W)]
        + [(6, 256, 256)]
        + [pltpu.SemaphoreType.DMA((1,))],
        [VMEM] * 5,
        32,
        [ANY] + [VMEM] * 7,
    )(ham, dens, wide, y_low, y_high)
    six, tile, rows = (2, 384, 384), (2, 2, 256, 256), (2, 4, W, 9 * W)
    return call(
        last_kernel,
        [ham.shape],
        [six] * 3
        + [tile] * 2
        + [(2, 2, 128, 256), rows, pltpu.SemaphoreType.DMA((2, 2))],
        [VMEM] * 13 + [ANY],
        32,
        [ANY],
        {13: 0},
    )(wide, y_low, y_high, x_low, x_high, c_low, *edges, out)[0]


def solution(mesh):
    return jax.shard_map(
        per_device,
        mesh=mesh,
        in_specs=(
            P("gx", "gy", None, None),
            P("gx", "gy", None, None),
            P("gx", "gy", None),
            P("gx", "gy", None),
        ),
        out_specs=P("gx", "gy", None, None),
        check_vma=False,
    )
```
